512 devices in a mesh: gx: 32 (over y, x, core), gy: 16 (over z).
Axes of the slice: x: 4, y: 4, z: 16, core: 2. Of those that a mesh axis runs over, the one named last changes fastest.
Arguments:
- pressure: float32 [512, 3, 8192], P('gx', None, 'gy'), may hold values from -6 to 6
- exchange_rates: float32 [512, 2, 8192], P('gx', None, 'gy'), may hold values from 0.05 to 0.45
- x_blocks: bfloat16 [512, 27, 8192], P('gx', None, 'gy')
- y_blocks: bfloat16 [512, 27, 8192], P('gx', None, 'gy')
- panels: bfloat16 [2048, 4, 512], P(('gx', 'gy')), may hold values from 0.19921875 to 2
- outlet_tiles: int32 [2048, 4], P(('gx', 'gy')), may hold values from 0 to 31, as said below
- outlet_counts: int32 [2048], P(('gx', 'gy')), may hold values from 1 to 4, as said below
- labels: int32 [512, 8192], P('gx', 'gy'), may hold values from 0 to 2047, as said below
Outputs:
- pressure_next: float32 [512, 3, 8192], P('gx', None, 'gy')
The draws below stay inside these ranges and needn't reach their ends.
Inputs may be any that keep to these rules, and one draw needn't show every extreme that they name: `outlet_tiles`: an outlet's 4 listed tiles are distinct; its first is the gx index of the device that holds it, each other entry is that index plus a nonzero offset modulo the number of tiles along gx. `outlet_counts`: the first outlet of every device feeds all 4 of its listed tiles. `labels`: A voxel's outlet is held by a device with the voxel's gy index and feeds the voxel's tile: x // 16 is among its first outlet_counts tiles.
All inputs are finite; a program needn't handle non-finite values.
Results may differ from the reference program's by a relative error of at most 0.0013.
Values may be sent and summed in bfloat16 or wider, within the bound.
No kernel may reach another device: no remote copies, remote signals or barrier semaphores. Data moves between devices by JAX's collectives and lax.ppermute only.
A program may use at most 64 MiB of HBM per device.

```python
import math
import jax
import jax.numpy as jnp
from jax import lax

CX = 16
CY = 32
NZ = 16
OUT_DEV = 4
TOP = 4
NX = 512
NY = 512
OUTLETS = 2048
N_GX = 32
N_GY = 16


def route_tables(key):
    offset_key, count_key = jax.random.split(key)
    candidates = jnp.arange(1, N_GX, dtype=jnp.int32)
    scores = jax.random.randint(offset_key, (N_GY, OUT_DEV, N_GX - 1), 0, 1024) * N_GX + candidates[None, None, :]
    first_slot = jnp.arange(OUT_DEV)[None, :, None] == 0
    scores = jnp.where(first_slot & (candidates[None, None, :] == N_GX // 2), -1, scores)
    order = jnp.argsort(scores, axis=-1, stable=True)
    picks = candidates[order[..., :TOP - 1]]
    offsets = jnp.concatenate([jnp.zeros((N_GY, OUT_DEV, 1), jnp.int32), picks], axis=-1)
    counts = jax.random.randint(count_key, (N_GX, N_GY, OUT_DEV), 1, TOP + 1)
    counts = jnp.where(jnp.arange(OUT_DEV)[None, None, :] == 0, TOP, counts)
    return (offsets, counts)


def draw_outlet_tiles(key, part):
    offsets, counts = route_tables(key)
    column = jnp.arange(N_GX)[:, None, None, None]
    tile_lists = jnp.remainder(column + offsets[None, :, :, :], N_GX)
    return tile_lists.reshape(OUTLETS, TOP).astype(jnp.int32)


def draw_outlet_counts(key, part):
    offsets, counts = route_tables(key)
    return counts.reshape(OUTLETS).astype(jnp.int32)


def draw_labels(key, part):
    offsets, counts = route_tables(key)
    key = jax.random.fold_in(key, 5)
    hop_key, member_key = jax.random.split(key)
    hops = jax.random.randint(hop_key, (NX, NY * NZ), 0, TOP)
    members = jax.random.randint(member_key, (NX, NY * NZ), 0, OUT_DEV)
    column = jnp.arange(NX)[:, None] // CX
    row_index = jnp.broadcast_to(jnp.arange(NY * NZ)[None, :] // (CY * NZ), (NX, NY * NZ))
    offset_here = offsets[row_index, members, hops]
    anchor = jnp.remainder(column - offset_here, N_GX)
    distant = (anchor * N_GY + row_index) * OUT_DEV + members
    own_outlet = (column * N_GY + row_index) * OUT_DEV + members
    live = counts.reshape(-1)[distant] > hops
    return jnp.where(live, distant, own_outlet).astype(jnp.int32)


def rotation(key, voxel_shape):
    axis_key, turn_key = jax.random.split(key)
    normals = jax.random.normal(axis_key, (3,) + voxel_shape)
    extent = jnp.sqrt(normals[0] * normals[0] + normals[1] * normals[1] + normals[2] * normals[2] + 1e-06)
    first = normals[0] / extent
    second = normals[1] / extent
    third = normals[2] / extent
    turn_angle = jax.random.uniform(turn_key, voxel_shape, minval=-0.6, maxval=0.6)
    cosine = jnp.cos(turn_angle)
    sine = jnp.sin(turn_angle)
    remainder_part = 1.0 - cosine
    return [[cosine + remainder_part * first * first, remainder_part * first * second - sine * third, remainder_part * first * third + sine * second], [remainder_part * second * first + sine * third, cosine + remainder_part * second * second, remainder_part * second * third - sine * first], [remainder_part * third * first - sine * second, remainder_part * third * second + sine * first, cosine + remainder_part * third * third]]


def decays(key, line_shape, voxel_shape, lowest, highest, sequence_length):
    baseline_key, jitter_key, spike_key = jax.random.split(key, 3)
    baseline_rate = jnp.exp(jax.random.uniform(baseline_key, line_shape, minval=math.log(lowest), maxval=math.log(highest)))
    voxel_rate = baseline_rate * jax.random.uniform(jitter_key, voxel_shape, minval=0.5, maxval=1.5)
    spike_events = jnp.where(jax.random.uniform(spike_key, voxel_shape) < 3.0 / sequence_length, 0.6, 1.0)
    return (jnp.exp(-voxel_rate) * spike_events, baseline_rate)


def block_table(key, line_shape, voxel_shape, lowest, highest, sequence_length):
    keys = jax.random.split(key, 12)
    forward_turn = rotation(keys[0], voxel_shape)
    backward_turn = rotation(keys[1], voxel_shape)
    forward_rows = [decays(keys[2 + row_number], line_shape, voxel_shape, lowest, highest, sequence_length) for row_number in range(3)]
    backward_rows = [decays(keys[7 + row_number], line_shape, voxel_shape, lowest, highest, sequence_length) for row_number in range(3)]
    forward_rate = (forward_rows[0][1] + forward_rows[1][1] + forward_rows[2][1]) / 3.0 + 1.5 / sequence_length
    backward_rate = (backward_rows[0][1] + backward_rows[1][1] + backward_rows[2][1]) / 3.0 + 1.5 / sequence_length
    entries = []
    for row_number in range(3):
        entries = entries + [forward_rows[row_number][0] * forward_turn[row_number][column_number] for column_number in range(3)]
    pivot_scale = jax.random.uniform(keys[5], voxel_shape, minval=0.5, maxval=1.5) * 2.0 * jnp.sqrt(forward_rate * backward_rate)
    coupling = jax.random.uniform(keys[6], (9,) + voxel_shape, minval=-0.3, maxval=0.3)
    for row_number in range(3):
        for column_number in range(3):
            if row_number == column_number:
                entries.append(pivot_scale)
            else:
                entries.append(pivot_scale * coupling[3 * row_number + column_number])
    for row_number in range(3):
        entries = entries + [backward_rows[row_number][0] * backward_turn[row_number][column_number] for column_number in range(3)]
    return jnp.stack(entries, axis=1)


def draw_x_blocks(key, part):
    key = jax.random.fold_in(key, 7)
    lowest, highest = (0.3 / NX, 0.06)
    table_now = block_table(key, (1, NY * NZ), (NX, NY * NZ), lowest, highest, NX)
    return table_now.astype(jnp.bfloat16)


def draw_y_blocks(key, part):
    key = jax.random.fold_in(key, 9)
    lowest, highest = (0.3 / NY, 0.06)
    table_now = block_table(key, (NX, 1, NZ), (NX, NY, NZ), lowest, highest, NY)
    return table_now.reshape(NX, 27, NY * NZ).astype(jnp.bfloat16)


def level_of(stream_key, shape, shards, least, top_value):
    level, own = 1.0, jax.random.fold_in(stream_key, 6)
    for axis_at, blocks in shards:
        draws = jnp.exp(jax.random.uniform(jax.random.fold_in(own, axis_at), (blocks,), jnp.float32, least / len(shards), top_value / len(shards)))
        level = level * jnp.repeat(draws, shape[axis_at] // blocks).reshape([-1 if axis == axis_at else 1 for axis in range(len(shape))])
    return level


def gaussian(rng, dims, scale, most, pieces=(), kind=jnp.bfloat16):
    loudness = level_of(rng, dims, pieces, -0.22, 0.18) if pieces else 1.0
    drawn = jax.random.normal(rng, dims, jnp.float32) * scale * loudness
    return jnp.minimum(jnp.maximum(drawn, -most), most).astype(kind)


def setup_inputs(seed: int = 0) -> dict:
    arg_keys = jax.random.split(jax.random.key(seed), 9)
    pressure = gaussian(arg_keys[0], (NX, 3, NY * NZ), 1.0, 6.0, ((0, 32), (2, 16)), jnp.float32)
    exchange_rates = jnp.clip(jnp.exp(math.log(0.45) - 2.1972245 * jax.random.uniform(arg_keys[1], (NX, 2, NY * NZ), jnp.float32) ** level_of(arg_keys[1], (NX, 2, NY * NZ), ((0, 32), (2, 16)), -0.2, 0.2)), 0.05, 0.45)
    x_blocks = draw_x_blocks(jax.random.fold_in(arg_keys[8], 71), 0)
    y_blocks = draw_y_blocks(jax.random.fold_in(arg_keys[8], 71), 0)
    panels = jnp.clip(jnp.exp(math.log(2.0) - 2.306499 * jax.random.uniform(arg_keys[4], (OUTLETS, TOP, CY * NZ), jnp.float32) ** level_of(arg_keys[4], (OUTLETS, TOP, CY * NZ), ((0, 512),), -0.2, 0.2)), 0.19921875, 2.0).astype(jnp.bfloat16)
    outlet_tiles = draw_outlet_tiles(jax.random.fold_in(arg_keys[8], 71), 0)
    outlet_counts = draw_outlet_counts(jax.random.fold_in(arg_keys[8], 71), 0)
    labels = draw_labels(jax.random.fold_in(arg_keys[8], 71), 0)
    return dict(pressure=pressure, exchange_rates=exchange_rates, x_blocks=x_blocks, y_blocks=y_blocks, panels=panels, outlet_tiles=outlet_tiles, outlet_counts=outlet_counts, labels=labels)


def matrix_vector(matrix, vector):
    return jnp.stack([matrix[3 * row_number] * vector[0] + matrix[3 * row_number + 1] * vector[1] + matrix[3 * row_number + 2] * vector[2] for row_number in range(3)])


def forward_pass(right_side, blocks, entering):
    def advance(carried, inputs):
        values, coefficients = inputs
        coefficients = coefficients.astype(jnp.float32)
        carried = matrix_vector(coefficients[0:9], carried) + matrix_vector(coefficients[9:18], values)
        return carried, carried
    return lax.scan(advance, entering, (right_side, blocks))[1]


def backward_pass(forward, blocks, entering):
    def retreat(carried, inputs):
        values, coefficients = inputs
        carried = matrix_vector(coefficients[18:27].astype(jnp.float32), carried) + values
        return carried, carried
    return lax.scan(retreat, entering, (forward, blocks), reverse=True)[1]


def depth_term(values):
    shape_now = values.shape
    column_grid = values.reshape(shape_now[:-1] + (shape_now[-1] // NZ, NZ))
    rising = column_grid[..., 1:] - column_grid[..., :-1]
    padding = [(0, 0)] * (column_grid.ndim - 1)
    spread = jnp.pad(rising, padding + [(0, 1)]) - jnp.pad(rising, padding + [(1, 0)])
    return spread.reshape(shape_now)


def explicit_step(pressure, exchange_rates, source):
    first = pressure[:, 0]
    second = pressure[:, 1]
    third = pressure[:, 2]
    inflow = exchange_rates[:, 0] * (first - second)
    outflow = exchange_rates[:, 1] * (second - third)
    return jnp.stack([first + source - inflow + 0.2 * depth_term(first), second + inflow - outflow + 0.2 * depth_term(second), third + outflow + 0.2 * depth_term(third)], axis=1)


def swap_rows(values):
    row_total, channels, combined = values.shape
    grid = values.reshape(row_total, channels, combined // NZ, NZ)
    return jnp.transpose(grid, (2, 1, 0, 3)).reshape(combined // NZ, channels, row_total * NZ)


def source_field(labels, outlet_tiles, outlet_counts, panels):
    tile_column = (jnp.arange(NX, dtype=jnp.int32) // CX)[:, None]
    local_column = (jnp.arange(NY * NZ, dtype=jnp.int32) % (CY * NZ))[None, :]
    counts_here = outlet_counts[labels]
    source = jnp.zeros(labels.shape, jnp.float32)
    for member in range(TOP):
        live = (outlet_tiles[:, member][labels] == tile_column) & (counts_here > member)
        picked = panels[:, member, :][labels, local_column].astype(jnp.float32)
        source = source + jnp.where(live, picked, 0.0)
    return source


def reference(pressure, exchange_rates, x_blocks, y_blocks, panels, outlet_tiles, outlet_counts, labels):
    source = source_field(labels, outlet_tiles, outlet_counts, panels)
    right_side = explicit_step(pressure, exchange_rates, source)
    empty_x = jnp.zeros((3, NY * NZ), jnp.float32)
    forward_x = forward_pass(right_side, x_blocks, empty_x)
    after_x = backward_pass(forward_x, x_blocks, empty_x)
    turned = swap_rows(after_x)
    turned_blocks = swap_rows(y_blocks)
    empty_y = jnp.zeros((3, NX * NZ), jnp.float32)
    forward_y = forward_pass(turned, turned_blocks, empty_y)
    return swap_rows(backward_pass(forward_y, turned_blocks, empty_y))
```

```python
import jax
import jax.numpy as jnp
from jax import lax
from jax.experimental import pallas as pl
from jax.experimental.pallas import tpu as pltpu
from jax.sharding import PartitionSpec as P

F32 = jnp.float32
BF16 = jnp.bfloat16
CX, CY, NZ = 16, 32, 16
TX, TY = 32, 16
NEAR = [[4 * q + k for k in range(4)] for q in range(4)]
FAR = [[4 * q + k for q in range(4)] for k in range(4)]
ROWS = 72
LANES = 128
GROUPS = 4
MAP = 33
VMEM = pl.BlockSpec(memory_space=pltpu.VMEM)
SMEM = pl.BlockSpec(memory_space=pltpu.SMEM)
PARAMS = pltpu.CompilerParams(vmem_limit_bytes=32 * 1024 * 1024)


def mm(a, b):
    return [
        a[3 * r] * b[c] + a[3 * r + 1] * b[3 + c] + a[3 * r + 2] * b[6 + c]
        for r in range(3)
        for c in range(3)
    ]


def mv(a, v):
    return [a[3 * r] * v[0] + a[3 * r + 1] * v[1] + a[3 * r + 2] * v[2] for r in range(3)]


def add(a, b):
    return [x + y for x, y in zip(a, b)]


def iota(shape, axis):
    return lax.broadcasted_iota(jnp.int32, shape, axis)


def swap_blocks(parts):
    block = iota(parts[0].shape, 1) // NZ
    for bit in (1, 2, 4):
        low = (block & bit) == 0
        fresh = list(parts)
        for i in range(8):
            if i & bit == 0:
                first, second = parts[i], parts[i | bit]
                fresh[i] = jnp.where(low, first, pltpu.roll(second, bit * NZ, 1))
                fresh[i | bit] = jnp.where(low, pltpu.roll(first, LANES - bit * NZ, 1), second)
        parts = fresh
    return parts


def load_blocks(blocks, coef):
    for k in range(27):
        rows = blocks[k].astype(F32)
        for g in range(GROUPS):
            coef[pl.ds(g * 432 + k * CX, CX), :] = rows[:, g * LANES : (g + 1) * LANES]


def x_matrix(coef, x, first):
    return [coef[pl.ds((first + k) * CX + x, GROUPS, stride=432), :] for k in range(9)]


def depth(v, z):
    up = jnp.where(z < NZ - 1, pltpu.roll(v, LANES - 1, 1) - v, 0.0)
    down = jnp.where(z > 0, v - pltpu.roll(v, 1, 1), 0.0)
    return up - down


def prepare_x(*refs):
    inputs, (packed, base) = refs[0:7], refs[7:9]
    buffers, arrived = refs[9:16], refs[16]
    coef, fields, prefix, feats, pan = refs[17:]
    copies = [pltpu.make_async_copy(inputs[k], buffers[k], arrived.at[k]) for k in range(7)]
    for copy in copies:
        copy.start()
    pressure, exchange, blocks, labels, panels, tiles, counts = buffers
    copies[0].wait()
    copies[1].wait()
    for g in range(GROUPS):
        cut = slice(g * LANES, (g + 1) * LANES)
        for k in range(3):
            fields[pl.ds(g * 128 + k * CX, CX), :] = pressure[k, :, cut]
        for x in range(CX):
            fields[pl.ds(g * 128 + 64 + x * 2, 2), :] = exchange[x, :, cut]
    z = iota((GROUPS, LANES), 1) & (NZ - 1)
    for x in range(CX):
        field = [fields[pl.ds(k * CX + x, GROUPS, stride=128), :] for k in range(3)]
        rates = [fields[pl.ds(64 + x * 2 + k, GROUPS, stride=128), :] for k in range(2)]
        inflow = rates[0] * (field[0] - field[1])
        outflow = rates[1] * (field[1] - field[2])
        base[x * 3] = field[0] - inflow + 0.2 * depth(field[0], z)
        base[x * 3 + 1] = field[1] + inflow - outflow + 0.2 * depth(field[1], z)
        base[x * 3 + 2] = field[2] + outflow + 0.2 * depth(field[2], z)
    for g in range(GROUPS):
        feats[pl.ds(g * 256 + 96, 160), :] = jnp.zeros((160, LANES), F32)
    copies[2].wait()
    load_blocks(blocks, coef)
    copies[3].wait()
    where_from = labels[...]
    where_from = (where_from // (TY * 4)) * 4 + (where_from & 3)
    where_from = where_from.astype(F32)
    for g in range(GROUPS):
        feats[pl.ds(g * 256 + 96, CX), :] = where_from[:, g * LANES : (g + 1) * LANES]

    u = x_matrix(coef, 0, 18)
    for x in range(1, CX):
        for k in range(9):
            prefix[x * 9 + k] = u[k]
        if x < CX - 1:
            u = mm(u, x_matrix(coef, x, 18))
    c_map = mm(u, x_matrix(coef, CX - 1, 18))

    def put(row, value):
        feats[pl.ds(row, GROUPS, stride=256), :] = value

    s, w = None, None
    b, e = None, None
    for x in reversed(range(CX)):
        ux = [prefix[x * 9 + k] for k in range(9)] if x > 0 else None
        if x == CX - 1:
            w = ux
        else:
            p = x_matrix(coef, x + 1, 0)
            s = p if s is None else mm(s, p)
            w = mm(w, p)
            if x > 0:
                w = add(w, ux)
            else:
                for k in (0, 4, 8):
                    w[k] = w[k] + 1.0
        gain = x_matrix(coef, x, 9)
        r = [base[x * 3 + k] for k in range(3)]
        column = [gain[0], gain[3], gain[6]]
        pushed = mv(gain, r)
        kb = column if s is None else mv(s, column)
        ke = mv(w, column)
        sb = pushed if s is None else mv(s, pushed)
        se = mv(w, pushed)
        b = sb if b is None else add(b, sb)
        e = se if e is None else add(e, se)
        for k in range(3):
            put(k * CX + x, kb[k])
            put((3 + k) * CX + x, ke[k])
    p = x_matrix(coef, 0, 0)
    values = mm(s, p) + c_map + mm(w, p) + b + e
    for k in range(MAP):
        high = values[k].astype(BF16).astype(F32)
        put(128 + k, high)
        put(128 + MAP + k, values[k] - high)

    for k in range(4, 7):
        copies[k].wait()
    for k in range(4):
        pan[pl.ds(k * 4, 4), :] = panels[k].astype(F32)
    row, column = iota((16, 4), 0), iota((16, 4), 1)
    listed = jnp.concatenate([jnp.broadcast_to(tiles[k : k + 1, :], (4, 4)) for k in range(4)], axis=0)
    limits = jnp.broadcast_to(counts[...], (16, 4))
    listed = jnp.sum(jnp.where(column == (row & 3), listed.astype(F32), 0.0), axis=1, keepdims=True)
    limits = jnp.sum(jnp.where(column == row // 4, limits.astype(F32), 0.0), axis=1, keepdims=True)
    routes = jnp.where((row[:, 0:1] & 3).astype(F32) < limits, listed, -1.0)
    routes = jnp.broadcast_to(routes, (16, LANES))
    routes = jnp.concatenate([routes] * 8, axis=0)
    lane = iota((LANES, LANES), 1)
    for g in range(GROUPS):
        rows = slice(g * LANES, (g + 1) * LANES)
        slab = pan[:, g * LANES : (g + 1) * LANES]
        pieces = [pltpu.roll(slab, (112 - i * NZ) % LANES, 1) if i < 7 else slab for i in range(8)]
        first = feats[pl.ds(g * 256, LANES), :].T
        first = jnp.where(lane >= 112, jnp.concatenate(pieces, axis=0), first)
        packed[rows, 0:LANES] = first.astype(BF16)
        second = feats[pl.ds(g * 256 + LANES, LANES), :].T
        second = jnp.where(lane == 72, routes, second)
        packed[rows, LANES : 2 * LANES] = second.astype(BF16)


def solve_x(received, answer, low, high, spread, target, out):
    for g in range(GROUPS):
        rows = slice(g * LANES, (g + 1) * LANES)
        low[rows, :] = received[rows, 0:LANES].astype(F32).T
        high[rows, :] = received[rows, LANES : 2 * LANES].astype(F32).T
    r_id, c_id = iota((LANES, LANES), 0), iota((LANES, LANES), 1)
    lane = iota((512, LANES), 1)
    copy_panel = ((r_id >= 112) & ((r_id - 112) == (c_id & (NZ - 1)))).astype(F32).astype(BF16)
    copy_route = (r_id == 72).astype(F32).astype(BF16)
    panel_part = received[:, 0:LANES].astype(F32)
    panel_part = jnp.where(lane >= 112, panel_part, 0.0).astype(BF16)
    route_part = received[:, LANES : 2 * LANES].astype(F32)
    route_part = jnp.where(lane == 72, route_part, 0.0).astype(BF16)
    spread[...] = jnp.dot(panel_part, copy_panel, preferred_element_type=F32)
    target[...] = jnp.dot(route_part, copy_route, preferred_element_type=F32)
    tile_lane = (c_id // NZ).astype(F32)
    for g in range(GROUPS):
        table = None
        for j in range(4):
            hit = target[pl.ds(j, LANES, stride=4), :] == tile_lane + 8.0 * g
            part = jnp.where(hit, spread[pl.ds(j, LANES, stride=4), :], 0.0)
            table = part if table is None else table + part
        position = low[pl.ds(g * LANES + 96, CX), :].astype(jnp.int32)
        found = []
        for half in range(2):
            place = position[half * 8 : half * 8 + 8, :]
            inner, outer = place & 7, place // 8
            picked = jnp.zeros((8, LANES), F32)
            for o in range(16):
                chosen = jnp.take_along_axis(table[o * 8 : o * 8 + 8, :], inner, axis=0)
                picked = jnp.where(outer == o, chosen, picked)
            found.append(picked)
        source = jnp.concatenate(found, axis=0)
        out[pl.ds(g * LANES + 24, CX), :] = source
        for k in range(6):
            response = low[pl.ds(g * LANES + k * CX, CX), :]
            extra = jnp.sum(response * source, axis=0, keepdims=True)
            at = pl.ds(g * LANES + 27 + k, 1)
            high[at, :] = high[at, :] + extra

    def value(k):
        return high[pl.ds(k, 8, stride=LANES), :] + high[pl.ds(MAP + k, 8, stride=LANES), :]

    lanes8 = iota((8, LANES), 1)
    tile = iota((8, LANES), 0) * 8 + lanes8 // NZ

    def before(v, d, fill):
        if d < 8:
            turned = pltpu.roll(v, d * NZ, 1)
            moved = jnp.where(lanes8 >= d * NZ, turned, pltpu.roll(turned, 1, 0))
        else:
            moved = pltpu.roll(v, d // 8, 0)
        return jnp.where(tile >= d, moved, fill)

    def after(v, d, fill):
        if d < 8:
            turned = pltpu.roll(v, LANES - d * NZ, 1)
            moved = jnp.where(lanes8 < LANES - d * NZ, turned, pltpu.roll(turned, 7, 0))
        else:
            moved = pltpu.roll(v, 8 - d // 8, 0)
        return jnp.where(tile + d < TX, moved, fill)

    def scan(matrix, vector, shift):
        for d in (1, 2, 4, 8, 16):
            vector_now = add(mv(matrix, [shift(v, d, 0.0) for v in vector]), vector)
            if d < 16:
                matrix = mm(matrix, [shift(m, d, 1.0 if k in (0, 4, 8) else 0.0) for k, m in enumerate(matrix)])
            vector = vector_now
        return [shift(v, 1, 0.0) for v in vector]

    enter = scan([value(k) for k in range(9)], [value(27 + k) for k in range(3)], before)
    pushed = add(mv([value(18 + k) for k in range(9)], enter), [value(30 + k) for k in range(3)])
    finish = scan([value(9 + k) for k in range(9)], pushed, after)
    for k, v in enumerate(enter + finish):
        for piece in range(3):
            part = v.astype(BF16).astype(F32)
            out[pl.ds(piece * 6 + k, 8, stride=LANES), :] = part
            v = v - part
    for g in range(GROUPS):
        rows = slice(g * LANES, (g + 1) * LANES)
        answer[rows, :] = out[rows, :].T.astype(BF16)


def prepare_y(blocks, turned, parts, whole, plain, coef):
    load_blocks(blocks, plain)
    for half in range(2):
        for g in range(GROUPS):
            rows = swap_blocks([plain[pl.ds(g * 432 + half * 8 + i, 27, stride=CX), :] for i in range(8)])
            for y in range(8):
                coef[pl.ds((g * 2 + half) * 256 + y * 32, 27), :] = rows[y]
    phi, u, d_map = None, None, None
    for y in range(8):
        block = [coef[pl.ds(y * 32 + k, 8, stride=256), :] for k in range(27)]
        for k in range(27):
            turned[y * 27 + k] = block[k]
        phi = block[0:9] if y == 0 else mm(block[0:9], phi)
        d_map = phi if y == 0 else add(d_map, mm(u, phi))
        u = block[18:27] if y == 0 else mm(u, block[18:27])
    for k, v in enumerate(phi + u + d_map):
        parts[pl.ds(k * 8, 8), :] = v
    a, c, d = [quarter(parts, 0, 9 * k, 9) for k in range(3)]
    for l in range(1, GROUPS):
        a_l, c_l, d_l = [quarter(parts, l, 9 * k, 9) for k in range(3)]
        d = add(mm(mm(c, d_l), a), d)
        a = mm(a_l, a)
        c = mm(c, c_l)
    for k, v in enumerate(a + c + d):
        whole[pl.ds(k * 2, 2), :] = v
    whole[pl.ds(54, 2), :] = jnp.zeros((2, LANES), F32)


def quarter(ref, l, first, count):
    return [ref[pl.ds((first + k) * 8 + l * 2, 2), :] for k in range(count)]


def finish_x(received, base, blocks, turned, parts, whole, sent, values, ends, coef, low, stage, lined):
    load_blocks(blocks, coef)
    for g in range(GROUPS):
        rows = slice(g * LANES, (g + 1) * LANES)
        low[rows, :] = received[rows, :].astype(F32).T

    def entry(k):
        rows = [low[pl.ds(piece * 6 + k, GROUPS, stride=LANES), :] for piece in range(3)]
        return rows[0] + rows[1] + rows[2]

    f = [entry(k) for k in range(3)]
    a = [entry(3 + k) for k in range(3)]
    forward = []
    for x in range(CX):
        source = low[pl.ds(24 + x, GROUPS, stride=LANES), :]
        r = [base[x * 3] + source, base[x * 3 + 1], base[x * 3 + 2]]
        f = add(mv(x_matrix(coef, x, 0), f), mv(x_matrix(coef, x, 9), r))
        forward.append(f)
    for x in reversed(range(CX)):
        a = add(mv(x_matrix(coef, x, 18), a), forward[x])
        for k in range(3):
            stage[pl.ds(x * 16 + k * 4, 4), :] = a[k]
    for half in range(2):
        rows = swap_blocks([stage[pl.ds((half * 8 + i) * 16, 16), :] for i in range(8)])
        for y in range(8):
            for k in range(3):
                lined[pl.ds(half * 24 + y * 3 + k, 4, stride=48), :] = rows[y][k * 4 : k * 4 + 4, :]
    f, forward = None, []
    for y in range(8):
        r = [lined[pl.ds(y * 3 + k, 8, stride=24), :] for k in range(3)]
        pushed = mv([turned[y * 27 + 9 + k] for k in range(9)], r)
        for k in range(3):
            values[y * 3 + k] = pushed[k]
        f = pushed if f is None else add(mv([turned[y * 27 + k] for k in range(9)], f), pushed)
        forward.append(f)
    a = None
    for y in reversed(range(8)):
        a = forward[y] if a is None else add(mv([turned[y * 27 + 18 + k] for k in range(9)], a), forward[y])
    for k, v in enumerate(forward[7] + a):
        ends[pl.ds(k * 8, 8), :] = v
    enter, f = [], None
    for l in range(GROUPS):
        enter.append(f)
        b_l = quarter(ends, l, 0, 3)
        f = b_l if f is None else add(mv(quarter(parts, l, 0, 9), f), b_l)
    a = None
    for l in reversed(range(GROUPS)):
        now = quarter(ends, l, 3, 3)
        if enter[l] is not None:
            now = add(now, mv(quarter(parts, l, 18, 9), enter[l]))
        a = now if a is None else add(mv(quarter(parts, l, 9, 9), a), now)
    put_map(sent, [whole[pl.ds(k * 2, 2), :] for k in range(27)] + f + a)


def put_map(sent, values):
    for k, v in enumerate(values):
        sent[pl.ds(k * 2, 2), :] = v
    sent[pl.ds(66, 6), :] = jnp.zeros((6, LANES), F32)
    for i in range(1, 4):
        sent[pl.ds(i * ROWS, ROWS), :] = sent[pl.ds(0, ROWS), :]


def get_map(ref, i):
    v = [ref[pl.ds(i * ROWS + k * 2, 2), :] for k in range(MAP)]
    return v[0:9], v[9:18], v[18:27], v[27:30], v[30:33]


def join_y(received, sent):
    a, c, d, b, e = get_map(received, 0)
    for i in range(1, 4):
        a1, c1, d1, b1, e1 = get_map(received, i)
        e = add(mv(c, add(mv(d1, b), e1)), e)
        d = add(mm(c, mm(d1, a)), d)
        b = add(mv(a1, b), b1)
        a = mm(a1, a)
        c = mm(c, c1)
    put_map(sent, a + c + d + b + e)


def narrow(received, mine, enter, finish):
    maps = [get_map(received, i) for i in range(4)]
    fs = [enter]
    for i in range(3):
        fs.append(add(mv(maps[i][0], fs[i]), maps[i][3]))
    ends = [None, None, None, finish]
    for i in (3, 2, 1):
        _, c, d, _, e = maps[i]
        ends[i - 1] = add(add(mv(c, ends[i]), mv(d, fs[i])), e)
    enter, finish = fs[0], ends[0]
    for i in range(1, 4):
        enter = [jnp.where(mine == i, n, o) for n, o in zip(fs[i], enter)]
        finish = [jnp.where(mine == i, n, o) for n, o in zip(ends[i], finish)]
    return enter, finish


def finish_y(place, near, far, values, ends, turned, parts, result, edge):
    me = place[0]
    zero = [jnp.zeros((2, LANES), F32) for _ in range(3)]
    enter, finish = narrow(far, me // 4, zero, zero)
    enter, finish = narrow(near, me % 4, enter, finish)
    f = enter
    inside = []
    for l in range(GROUPS):
        inside.append(f)
        for k in range(3):
            edge[pl.ds(k * 8 + l * 2, 2), :] = f[k]
        if l < GROUPS - 1:
            f = add(mv(quarter(parts, l, 0, 9), f), quarter(ends, l, 0, 3))
    a = finish
    for l in reversed(range(GROUPS)):
        for k in range(3):
            edge[pl.ds(24 + k * 8 + l * 2, 2), :] = a[k]
        if l > 0:
            a = add(
                add(mv(quarter(parts, l, 9, 9), a), mv(quarter(parts, l, 18, 9), inside[l])),
                quarter(ends, l, 3, 3),
            )
    f = [edge[pl.ds(k * 8, 8), :] for k in range(3)]
    a = [edge[pl.ds(24 + k * 8, 8), :] for k in range(3)]
    forward = []
    for y in range(8):
        f = add(mv([turned[y * 27 + k] for k in range(9)], f), [values[y * 3 + k] for k in range(3)])
        forward.append(f)
    solved = [None] * 8
    for y in reversed(range(8)):
        a = add(mv([turned[y * 27 + 18 + k] for k in range(9)], a), forward[y])
        solved[y] = a
    for k in range(3):
        rows = swap_blocks([solved[y][k] for y in range(8)])
        for x in range(8):
            for g in range(GROUPS):
                for half in range(2):
                    at = g * 2 + half
                    result[k, pl.ds(half * 8 + x, 1), g * LANES : (g + 1) * LANES] = rows[x][at : at + 1, :]


def body(pressure, exchange_rates, x_blocks, y_blocks, panels, outlet_tiles, outlet_counts, labels):
    shape = jax.ShapeDtypeStruct
    pressure, x_blocks, y_blocks = [jnp.transpose(v, (1, 0, 2)) for v in (pressure, x_blocks, y_blocks)]
    inputs = (pressure, exchange_rates, x_blocks, labels, panels, outlet_tiles, outlet_counts.reshape(1, 4))
    packed, base = pl.pallas_call(
        prepare_x,
        out_shape=(shape((512, 256), BF16), shape((CX * 3, GROUPS, LANES), F32)),
        in_specs=[pl.BlockSpec(memory_space=pltpu.HBM)] * 7,
        out_specs=(VMEM, VMEM),
        scratch_shapes=[pltpu.VMEM(v.shape, v.dtype) for v in inputs]
        + [
            pltpu.SemaphoreType.DMA((7,)),
            pltpu.VMEM((1728, LANES), F32),
            pltpu.VMEM((512, LANES), F32),
            pltpu.VMEM((CX * 9, GROUPS, LANES), F32),
            pltpu.VMEM((1024, LANES), F32),
            pltpu.VMEM((16, 512), F32),
        ],
        name="prepare_x",
    )(*inputs)
    received = lax.all_to_all(packed, "gx", split_axis=0, concat_axis=0, tiled=True)
    turned, parts, whole = pl.pallas_call(
        prepare_y,
        out_shape=(
            shape((8 * 27, 8, LANES), F32),
            shape((27 * 8, LANES), F32),
            shape((56, LANES), F32),
        ),
        in_specs=[VMEM],
        out_specs=(VMEM,) * 3,
        scratch_shapes=[pltpu.VMEM((1728, LANES), F32), pltpu.VMEM((2048, LANES), F32)],
        compiler_params=PARAMS,
        name="prepare_y",
    )(y_blocks)
    answer = pl.pallas_call(
        solve_x,
        out_shape=shape((512, LANES), BF16),
        in_specs=[VMEM],
        out_specs=VMEM,
        scratch_shapes=[
            pltpu.VMEM((512, LANES), F32),
            pltpu.VMEM((1024, LANES), F32),
            pltpu.VMEM((512, LANES), F32),
            pltpu.VMEM((512, LANES), F32),
            pltpu.VMEM((1024, LANES), F32),
        ],
        compiler_params=PARAMS,
        name="solve_x",
    )(received)
    entries = lax.all_to_all(answer, "gx", split_axis=0, concat_axis=0, tiled=True)
    sent, values, ends = pl.pallas_call(
        finish_x,
        out_shape=(
            shape((4 * ROWS, LANES), F32),
            shape((24, 8, LANES), F32),
            shape((48, LANES), F32),
        ),
        in_specs=[VMEM] * 6,
        out_specs=(VMEM,) * 3,
        scratch_shapes=[
            pltpu.VMEM((1728, LANES), F32),
            pltpu.VMEM((512, LANES), F32),
            pltpu.VMEM((256, LANES), F32),
            pltpu.VMEM((192, LANES), F32),
        ],
        compiler_params=PARAMS,
        name="finish_x",
    )(entries, base, x_blocks, turned, parts, whole)
    near = lax.all_to_all(sent, "gy", split_axis=0, concat_axis=0, tiled=True, axis_index_groups=NEAR)
    joined = pl.pallas_call(
        join_y,
        out_shape=shape((4 * ROWS, LANES), F32),
        in_specs=[VMEM],
        out_specs=VMEM,
        compiler_params=PARAMS,
        name="join_y",
    )(near)
    far = lax.all_to_all(joined, "gy", split_axis=0, concat_axis=0, tiled=True, axis_index_groups=FAR)
    place = lax.axis_index("gy").astype(jnp.int32).reshape(1)
    result = pl.pallas_call(
        finish_y,
        out_shape=shape((3, CX, 512), F32),
        in_specs=[SMEM] + [VMEM] * 6,
        out_specs=VMEM,
        scratch_shapes=[pltpu.VMEM((48, LANES), F32)],
        compiler_params=PARAMS,
        name="finish_y",
    )(place, near, far, values, ends, turned, parts)
    return jnp.transpose(result, (1, 0, 2))


def solution(mesh):
    in_specs = (
        P("gx", None, "gy"),
        P("gx", None, "gy"),
        P("gx", None, "gy"),
        P("gx", None, "gy"),
        P(("gx", "gy"), None, None),
        P(("gx", "gy"), None),
        P(("gx", "gy")),
        P("gx", "gy"),
    )
    out_specs = P("gx", None, "gy")
    return jax.shard_map(body, mesh=mesh, in_specs=in_specs, out_specs=out_specs, check_vma=False)
```

```python
import jax
import jax.numpy as jnp
from jax import lax
from jax.experimental import pallas as pl
from jax.experimental.pallas import tpu as pltpu
from jax.sharding import PartitionSpec as P

F32 = jnp.float32
BF16 = jnp.bfloat16
CX, CY, NZ = 16, 32, 16
TX, TY = 32, 16
NEAR = [[4 * q + k for k in range(4)] for q in range(4)]
FAR = [[4 * q + k for q in range(4)] for k in range(4)]
ROWS = 72
LANES = 128
GROUPS = 4
MAP = 33
VMEM = pl.BlockSpec(memory_space=pltpu.VMEM)
SMEM = pl.BlockSpec(memory_space=pltpu.SMEM)
PARAMS = pltpu.CompilerParams(vmem_limit_bytes=32 * 1024 * 1024)


def mm(a, b):
    return [
        a[3 * r] * b[c] + a[3 * r + 1] * b[3 + c] + a[3 * r + 2] * b[6 + c]
        for r in range(3)
        for c in range(3)
    ]


def mv(a, v):
    return [a[3 * r] * v[0] + a[3 * r + 1] * v[1] + a[3 * r + 2] * v[2] for r in range(3)]


def add(a, b):
    return [x + y for x, y in zip(a, b)]


def iota(shape, axis):
    return lax.broadcasted_iota(jnp.int32, shape, axis)


def swap_blocks(parts):
    block = iota(parts[0].shape, 1) // NZ
    for bit in (1, 2, 4):
        low = (block & bit) == 0
        fresh = list(parts)
        for i in range(8):
            if i & bit == 0:
                first, second = parts[i], parts[i | bit]
                fresh[i] = jnp.where(low, first, pltpu.roll(second, bit * NZ, 1))
                fresh[i | bit] = jnp.where(low, pltpu.roll(first, LANES - bit * NZ, 1), second)
        parts = fresh
    return parts


def load_blocks(blocks, coef):
    for k in range(27):
        rows = blocks[k].astype(F32)
        for g in range(GROUPS):
            coef[pl.ds(g * 432 + k * CX, CX), :] = rows[:, g * LANES : (g + 1) * LANES]


def x_matrix(coef, x, first):
    return [coef[pl.ds((first + k) * CX + x, GROUPS, stride=432), :] for k in range(9)]


def depth(v, z):
    up = jnp.where(z < NZ - 1, pltpu.roll(v, LANES - 1, 1) - v, 0.0)
    down = jnp.where(z > 0, v - pltpu.roll(v, 1, 1), 0.0)
    return up - down


def prepare_x(*refs):
    inputs, (packed, base) = refs[0:7], refs[7:9]
    buffers, arrived = refs[9:16], refs[16]
    coef, fields, prefix, feats, pan = refs[17:]
    copies = [pltpu.make_async_copy(inputs[k], buffers[k], arrived.at[k]) for k in range(7)]
    for copy in copies:
        copy.start()
    pressure, exchange, blocks, labels, panels, tiles, counts = buffers
    copies[0].wait()
    copies[1].wait()
    for g in range(GROUPS):
        cut = slice(g * LANES, (g + 1) * LANES)
        for k in range(3):
            fields[pl.ds(g * 128 + k * CX, CX), :] = pressure[k, :, cut]
        for x in range(CX):
            fields[pl.ds(g * 128 + 64 + x * 2, 2), :] = exchange[x, :, cut]
    z = iota((GROUPS, LANES), 1) & (NZ - 1)
    for x in range(CX):
        field = [fields[pl.ds(k * CX + x, GROUPS, stride=128), :] for k in range(3)]
        rates = [fields[pl.ds(64 + x * 2 + k, GROUPS, stride=128), :] for k in range(2)]
        inflow = rates[0] * (field[0] - field[1])
        outflow = rates[1] * (field[1] - field[2])
        base[x * 3] = field[0] - inflow + 0.2 * depth(field[0], z)
        base[x * 3 + 1] = field[1] + inflow - outflow + 0.2 * depth(field[1], z)
        base[x * 3 + 2] = field[2] + outflow + 0.2 * depth(field[2], z)
    for g in range(GROUPS):
        feats[pl.ds(g * 256 + 96, 160), :] = jnp.zeros((160, LANES), F32)
    copies[2].wait()
    load_blocks(blocks, coef)
    copies[3].wait()
    where_from = labels[...]
    where_from = (where_from // (TY * 4)) * 4 + (where_from & 3)
    where_from = where_from.astype(F32)
    for g in range(GROUPS):
        feats[pl.ds(g * 256 + 96, CX), :] = where_from[:, g * LANES : (g + 1) * LANES]

    u = x_matrix(coef, 0, 18)
    for x in range(1, CX):
        for k in range(9):
            prefix[x * 9 + k] = u[k]
        if x < CX - 1:
            u = mm(u, x_matrix(coef, x, 18))
    c_map = mm(u, x_matrix(coef, CX - 1, 18))

    def put(row, value):
        feats[pl.ds(row, GROUPS, stride=256), :] = value

    s, w = None, None
    b, e = None, None
    for x in reversed(range(CX)):
        ux = [prefix[x * 9 + k] for k in range(9)] if x > 0 else None
        if x == CX - 1:
            w = ux
        else:
            p = x_matrix(coef, x + 1, 0)
            s = p if s is None else mm(s, p)
            w = mm(w, p)
            if x > 0:
                w = add(w, ux)
            else:
                for k in (0, 4, 8):
                    w[k] = w[k] + 1.0
        gain = x_matrix(coef, x, 9)
        r = [base[x * 3 + k] for k in range(3)]
        column = [gain[0], gain[3], gain[6]]
        pushed = mv(gain, r)
        kb = column if s is None else mv(s, column)
        ke = mv(w, column)
        sb = pushed if s is None else mv(s, pushed)
        se = mv(w, pushed)
        b = sb if b is None else add(b, sb)
        e = se if e is None else add(e, se)
        for k in range(3):
            put(k * CX + x, kb[k])
            put((3 + k) * CX + x, ke[k])
    p = x_matrix(coef, 0, 0)
    values = mm(s, p) + c_map + mm(w, p) + b + e
    for k in range(MAP):
        high = values[k].astype(BF16).astype(F32)
        put(128 + k, high)
        put(128 + MAP + k, values[k] - high)

    for k in range(4, 7):
        copies[k].wait()
    for k in range(4):
        pan[pl.ds(k * 4, 4), :] = panels[k].astype(F32)
    row, column = iota((16, 4), 0), iota((16, 4), 1)
    listed = jnp.concatenate([jnp.broadcast_to(tiles[k : k + 1, :], (4, 4)) for k in range(4)], axis=0)
    limits = jnp.broadcast_to(counts[...], (16, 4))
    listed = jnp.sum(jnp.where(column == (row & 3), listed.astype(F32), 0.0), axis=1, keepdims=True)
    limits = jnp.sum(jnp.where(column == row // 4, limits.astype(F32), 0.0), axis=1, keepdims=True)
    routes = jnp.where((row[:, 0:1] & 3).astype(F32) < limits, listed, -1.0)
    routes = jnp.broadcast_to(routes, (16, LANES))
    routes = jnp.concatenate([routes] * 8, axis=0)
    lane = iota((LANES, LANES), 1)
    for g in range(GROUPS):
        rows = slice(g * LANES, (g + 1) * LANES)
        slab = pan[:, g * LANES : (g + 1) * LANES]
        pieces = [pltpu.roll(slab, (112 - i * NZ) % LANES, 1) if i < 7 else slab for i in range(8)]
        first = feats[pl.ds(g * 256, LANES), :].T
        first = jnp.where(lane >= 112, jnp.concatenate(pieces, axis=0), first)
        packed[rows, 0:LANES] = first.astype(BF16)
        second = feats[pl.ds(g * 256 + LANES, LANES), :].T
        second = jnp.where(lane == 72, routes, second)
        packed[rows, LANES : 2 * LANES] = second.astype(BF16)


def solve_x(received, answer, low, high, spread, target, out):
    for g in range(GROUPS):
        rows = slice(g * LANES, (g + 1) * LANES)
        low[rows, :] = received[rows, 0:LANES].astype(F32).T
        high[rows, :] = received[rows, LANES : 2 * LANES].astype(F32).T
    r_id, c_id = iota((LANES, LANES), 0), iota((LANES, LANES), 1)
    lane = iota((512, LANES), 1)
    copy_panel = ((r_id >= 112) & ((r_id - 112) == (c_id & (NZ - 1)))).astype(F32).astype(BF16)
    copy_route = (r_id == 72).astype(F32).astype(BF16)
    panel_part = received[:, 0:LANES].astype(F32)
    panel_part = jnp.where(lane >= 112, panel_part, 0.0).astype(BF16)
    route_part = received[:, LANES : 2 * LANES].astype(F32)
    route_part = jnp.where(lane == 72, route_part, 0.0).astype(BF16)
    spread[...] = jnp.dot(panel_part, copy_panel, preferred_element_type=F32)
    target[...] = jnp.dot(route_part, copy_route, preferred_element_type=F32)
    tile_lane = (c_id // NZ).astype(F32)
    for g in range(GROUPS):
        table = None
        for j in range(4):
            hit = target[pl.ds(j, LANES, stride=4), :] == tile_lane + 8.0 * g
            part = jnp.where(hit, spread[pl.ds(j, LANES, stride=4), :], 0.0)
            table = part if table is None else table + part
        position = low[pl.ds(g * LANES + 96, CX), :].astype(jnp.int32)
        found = []
        for half in range(2):
            place = position[half * 8 : half * 8 + 8, :]
            inner, outer = place & 7, place // 8
            picked = jnp.zeros((8, LANES), F32)
            for o in range(16):
                chosen = jnp.take_along_axis(table[o * 8 : o * 8 + 8, :], inner, axis=0)
                picked = jnp.where(outer == o, chosen, picked)
            found.append(picked)
        source = jnp.concatenate(found, axis=0)
        out[pl.ds(g * LANES + 24, CX), :] = source
        for k in range(6):
            response = low[pl.ds(g * LANES + k * CX, CX), :]
            extra = jnp.sum(response * source, axis=0, keepdims=True)
            at = pl.ds(g * LANES + 27 + k, 1)
            high[at, :] = high[at, :] + extra

    def value(k):
        return high[pl.ds(k, 8, stride=LANES), :] + high[pl.ds(MAP + k, 8, stride=LANES), :]

    lanes8 = iota((8, LANES), 1)
    tile = iota((8, LANES), 0) * 8 + lanes8 // NZ

    def before(v, d, fill):
        if d < 8:
            turned = pltpu.roll(v, d * NZ, 1)
            moved = jnp.where(lanes8 >= d * NZ, turned, pltpu.roll(turned, 1, 0))
        else:
            moved = pltpu.roll(v, d // 8, 0)
        return jnp.where(tile >= d, moved, fill)

    def after(v, d, fill):
        if d < 8:
            turned = pltpu.roll(v, LANES - d * NZ, 1)
            moved = jnp.where(lanes8 < LANES - d * NZ, turned, pltpu.roll(turned, 7, 0))
        else:
            moved = pltpu.roll(v, 8 - d // 8, 0)
        return jnp.where(tile + d < TX, moved, fill)

    def scan(matrix, vector, shift):
        for d in (1, 2, 4, 8, 16):
            vector_now = add(mv(matrix, [shift(v, d, 0.0) for v in vector]), vector)
            if d < 16:
                matrix = mm(matrix, [shift(m, d, 1.0 if k in (0, 4, 8) else 0.0) for k, m in enumerate(matrix)])
            vector = vector_now
        return [shift(v, 1, 0.0) for v in vector]

    enter = scan([value(k) for k in range(9)], [value(27 + k) for k in range(3)], before)
    pushed = add(mv([value(18 + k) for k in range(9)], enter), [value(30 + k) for k in range(3)])
    finish = scan([value(9 + k) for k in range(9)], pushed, after)
    for k, v in enumerate(enter + finish):
        for piece in range(3):
            part = v.astype(BF16).astype(F32)
            out[pl.ds(piece * 6 + k, 8, stride=LANES), :] = part
            v = v - part
    for g in range(GROUPS):
        rows = slice(g * LANES, (g + 1) * LANES)
        answer[rows, :] = out[rows, :].T.astype(BF16)


def prepare_y(place, blocks, turned, parts, whole, spot, plain, coef):
    spot[...] = jnp.full((8, LANES), place[0], jnp.int32)
    load_blocks(blocks, plain)
    for half in range(2):
        for g in range(GROUPS):
            rows = swap_blocks([plain[pl.ds(g * 432 + half * 8 + i, 27, stride=CX), :] for i in range(8)])
            for y in range(8):
                coef[pl.ds((g * 2 + half) * 256 + y * 32, 27), :] = rows[y]
    phi, u, d_map = None, None, None
    for y in range(8):
        block = [coef[pl.ds(y * 32 + k, 8, stride=256), :] for k in range(27)]
        for k in range(27):
            turned[y * 27 + k] = block[k]
        phi = block[0:9] if y == 0 else mm(block[0:9], phi)
        d_map = phi if y == 0 else add(d_map, mm(u, phi))
        u = block[18:27] if y == 0 else mm(u, block[18:27])
    for k, v in enumerate(phi + u + d_map):
        parts[pl.ds(k * 8, 8), :] = v
    a, c, d = [quarter(parts, 0, 9 * k, 9) for k in range(3)]
    for l in range(1, GROUPS):
        a_l, c_l, d_l = [quarter(parts, l, 9 * k, 9) for k in range(3)]
        d = add(mm(mm(c, d_l), a), d)
        a = mm(a_l, a)
        c = mm(c, c_l)
    for k, v in enumerate(a + c + d):
        whole[pl.ds(k * 2, 2), :] = v
    whole[pl.ds(54, 2), :] = jnp.zeros((2, LANES), F32)


def quarter(ref, l, first, count):
    return [ref[pl.ds((first + k) * 8 + l * 2, 2), :] for k in range(count)]


def finish_x(received, base, blocks, turned, parts, whole, sent, values, ends, coef, low, stage, lined):
    load_blocks(blocks, coef)
    for g in range(GROUPS):
        rows = slice(g * LANES, (g + 1) * LANES)
        low[rows, :] = received[rows, :].astype(F32).T

    def entry(k):
        rows = [low[pl.ds(piece * 6 + k, GROUPS, stride=LANES), :] for piece in range(3)]
        return rows[0] + rows[1] + rows[2]

    f = [entry(k) for k in range(3)]
    a = [entry(3 + k) for k in range(3)]
    forward = []
    for x in range(CX):
        source = low[pl.ds(24 + x, GROUPS, stride=LANES), :]
        r = [base[x * 3] + source, base[x * 3 + 1], base[x * 3 + 2]]
        f = add(mv(x_matrix(coef, x, 0), f), mv(x_matrix(coef, x, 9), r))
        forward.append(f)
    for x in reversed(range(CX)):
        a = add(mv(x_matrix(coef, x, 18), a), forward[x])
        for k in range(3):
            stage[pl.ds(x * 16 + k * 4, 4), :] = a[k]
    for half in range(2):
        rows = swap_blocks([stage[pl.ds((half * 8 + i) * 16, 16), :] for i in range(8)])
        for y in range(8):
            for k in range(3):
                lined[pl.ds(half * 24 + y * 3 + k, 4, stride=48), :] = rows[y][k * 4 : k * 4 + 4, :]
    f, forward = None, []
    for y in range(8):
        r = [lined[pl.ds(y * 3 + k, 8, stride=24), :] for k in range(3)]
        pushed = mv([turned[y * 27 + 9 + k] for k in range(9)], r)
        for k in range(3):
            values[y * 3 + k] = pushed[k]
        f = pushed if f is None else add(mv([turned[y * 27 + k] for k in range(9)], f), pushed)
        forward.append(f)
    a = None
    for y in reversed(range(8)):
        a = forward[y] if a is None else add(mv([turned[y * 27 + 18 + k] for k in range(9)], a), forward[y])
    for k, v in enumerate(forward[7] + a):
        ends[pl.ds(k * 8, 8), :] = v
    enter, f = [], None
    for l in range(GROUPS):
        enter.append(f)
        b_l = quarter(ends, l, 0, 3)
        f = b_l if f is None else add(mv(quarter(parts, l, 0, 9), f), b_l)
    a = None
    for l in reversed(range(GROUPS)):
        now = quarter(ends, l, 3, 3)
        if enter[l] is not None:
            now = add(now, mv(quarter(parts, l, 18, 9), enter[l]))
        a = now if a is None else add(mv(quarter(parts, l, 9, 9), a), now)
    put_map(sent, [whole[pl.ds(k * 2, 2), :] for k in range(27)] + f + a)


def put_map(sent, values):
    for k, v in enumerate(values):
        sent[pl.ds(k * 2, 2), :] = v
    sent[pl.ds(66, 6), :] = jnp.zeros((6, LANES), F32)
    for i in range(1, 4):
        sent[pl.ds(i * ROWS, ROWS), :] = sent[pl.ds(0, ROWS), :]


def get_map(ref, i):
    v = [ref[pl.ds(i * ROWS + k * 2, 2), :] for k in range(MAP)]
    return v[0:9], v[9:18], v[18:27], v[27:30], v[30:33]


def join_y(received, sent):
    a, c, d, b, e = get_map(received, 0)
    for i in range(1, 4):
        a1, c1, d1, b1, e1 = get_map(received, i)
        e = add(mv(c, add(mv(d1, b), e1)), e)
        d = add(mm(c, mm(d1, a)), d)
        b = add(mv(a1, b), b1)
        a = mm(a1, a)
        c = mm(c, c1)
    put_map(sent, a + c + d + b + e)


def narrow(received, mine, enter, finish):
    maps = [get_map(received, i) for i in range(4)]
    fs = [enter]
    for i in range(3):
        fs.append(add(mv(maps[i][0], fs[i]), maps[i][3]))
    ends = [None, None, None, finish]
    for i in (3, 2, 1):
        _, c, d, _, e = maps[i]
        ends[i - 1] = add(add(mv(c, ends[i]), mv(d, fs[i])), e)
    enter, finish = fs[0], ends[0]
    for i in range(1, 4):
        enter = [jnp.where(mine == i, n, o) for n, o in zip(fs[i], enter)]
        finish = [jnp.where(mine == i, n, o) for n, o in zip(ends[i], finish)]
    return enter, finish


def finish_y(spot, near, far, values, ends, turned, parts, result, edge):
    me = spot[0:2, :]
    zero = [jnp.zeros((2, LANES), F32) for _ in range(3)]
    enter, finish = narrow(far, me // 4, zero, zero)
    enter, finish = narrow(near, me % 4, enter, finish)
    f = enter
    inside = []
    for l in range(GROUPS):
        inside.append(f)
        for k in range(3):
            edge[pl.ds(k * 8 + l * 2, 2), :] = f[k]
        if l < GROUPS - 1:
            f = add(mv(quarter(parts, l, 0, 9), f), quarter(ends, l, 0, 3))
    a = finish
    for l in reversed(range(GROUPS)):
        for k in range(3):
            edge[pl.ds(24 + k * 8 + l * 2, 2), :] = a[k]
        if l > 0:
            a = add(
                add(mv(quarter(parts, l, 9, 9), a), mv(quarter(parts, l, 18, 9), inside[l])),
                quarter(ends, l, 3, 3),
            )
    f = [edge[pl.ds(k * 8, 8), :] for k in range(3)]
    a = [edge[pl.ds(24 + k * 8, 8), :] for k in range(3)]
    forward = []
    for y in range(8):
        f = add(mv([turned[y * 27 + k] for k in range(9)], f), [values[y * 3 + k] for k in range(3)])
        forward.append(f)
    solved = [None] * 8
    for y in reversed(range(8)):
        a = add(mv([turned[y * 27 + 18 + k] for k in range(9)], a), forward[y])
        solved[y] = a
    for k in range(3):
        rows = swap_blocks([solved[y][k] for y in range(8)])
        for x in range(8):
            for g in range(GROUPS):
                for half in range(2):
                    at = g * 2 + half
                    result[k, pl.ds(half * 8 + x, 1), g * LANES : (g + 1) * LANES] = rows[x][at : at + 1, :]


def body(pressure, exchange_rates, x_blocks, y_blocks, panels, outlet_tiles, outlet_counts, labels):
    shape = jax.ShapeDtypeStruct
    pressure, x_blocks, y_blocks = [jnp.transpose(v, (1, 0, 2)) for v in (pressure, x_blocks, y_blocks)]
    inputs = (pressure, exchange_rates, x_blocks, labels, panels, outlet_tiles, outlet_counts.reshape(1, 4))
    place = lax.axis_index("gy").astype(jnp.int32).reshape(1)
    packed, base = pl.pallas_call(
        prepare_x,
        out_shape=(shape((512, 256), BF16), shape((CX * 3, GROUPS, LANES), F32)),
        in_specs=[pl.BlockSpec(memory_space=pltpu.HBM)] * 7,
        out_specs=(VMEM,) * 2,
        scratch_shapes=[pltpu.VMEM(v.shape, v.dtype) for v in inputs]
        + [
            pltpu.SemaphoreType.DMA((7,)),
            pltpu.VMEM((1728, LANES), F32),
            pltpu.VMEM((512, LANES), F32),
            pltpu.VMEM((CX * 9, GROUPS, LANES), F32),
            pltpu.VMEM((1024, LANES), F32),
            pltpu.VMEM((16, 512), F32),
        ],
        name="prepare_x",
    )(*inputs)
    received = lax.all_to_all(packed, "gx", split_axis=0, concat_axis=0, tiled=True)
    turned, parts, whole, spot = pl.pallas_call(
        prepare_y,
        out_shape=(
            shape((8 * 27, 8, LANES), F32),
            shape((27 * 8, LANES), F32),
            shape((56, LANES), F32),
            shape((8, LANES), jnp.int32),
        ),
        in_specs=[SMEM, VMEM],
        out_specs=(VMEM,) * 4,
        scratch_shapes=[pltpu.VMEM((1728, LANES), F32), pltpu.VMEM((2048, LANES), F32)],
        compiler_params=PARAMS,
        name="prepare_y",
    )(place, y_blocks)
    received, whole = lax.optimization_barrier((received, whole))
    answer = pl.pallas_call(
        solve_x,
        out_shape=shape((512, LANES), BF16),
        in_specs=[VMEM],
        out_specs=VMEM,
        scratch_shapes=[
            pltpu.VMEM((512, LANES), F32),
            pltpu.VMEM((1024, LANES), F32),
            pltpu.VMEM((512, LANES), F32),
            pltpu.VMEM((512, LANES), F32),
            pltpu.VMEM((1024, LANES), F32),
        ],
        compiler_params=PARAMS,
        name="solve_x",
    )(received)
    entries = lax.all_to_all(answer, "gx", split_axis=0, concat_axis=0, tiled=True)
    sent, values, ends = pl.pallas_call(
        finish_x,
        out_shape=(
            shape((4 * ROWS, LANES), F32),
            shape((24, 8, LANES), F32),
            shape((48, LANES), F32),
        ),
        in_specs=[VMEM] * 6,
        out_specs=(VMEM,) * 3,
        scratch_shapes=[
            pltpu.VMEM((1728, LANES), F32),
            pltpu.VMEM((512, LANES), F32),
            pltpu.VMEM((256, LANES), F32),
            pltpu.VMEM((192, LANES), F32),
        ],
        compiler_params=PARAMS,
        name="finish_x",
    )(entries, base, x_blocks, turned, parts, whole)
    near = lax.all_to_all(sent, "gy", split_axis=0, concat_axis=0, tiled=True, axis_index_groups=NEAR)
    joined = pl.pallas_call(
        join_y,
        out_shape=shape((4 * ROWS, LANES), F32),
        in_specs=[VMEM],
        out_specs=VMEM,
        compiler_params=PARAMS,
        name="join_y",
    )(near)
    far = lax.all_to_all(joined, "gy", split_axis=0, concat_axis=0, tiled=True, axis_index_groups=FAR)
    result = pl.pallas_call(
        finish_y,
        out_shape=shape((3, CX, 512), F32),
        in_specs=[VMEM] * 7,
        out_specs=VMEM,
        scratch_shapes=[pltpu.VMEM((48, LANES), F32)],
        compiler_params=PARAMS,
        name="finish_y",
    )(spot, near, far, values, ends, turned, parts)
    return jnp.transpose(result, (1, 0, 2))


def solution(mesh):
    in_specs = (
        P("gx", None, "gy"),
        P("gx", None, "gy"),
        P("gx", None, "gy"),
        P("gx", None, "gy"),
        P(("gx", "gy"), None, None),
        P(("gx", "gy"), None),
        P(("gx", "gy")),
        P("gx", "gy"),
    )
    out_specs = P("gx", None, "gy")
    return jax.shard_map(body, mesh=mesh, in_specs=in_specs, out_specs=out_specs, check_vma=False)
```

```python
import jax
import jax.numpy as jnp
from jax import lax
from jax.experimental import pallas as pl
from jax.experimental.pallas import tpu as pltpu
from jax.sharding import PartitionSpec as P

F32 = jnp.float32
BF16 = jnp.bfloat16
CX, CY, NZ = 16, 32, 16
TX, TY = 32, 16
NEAR_ORDER, FAR_ORDER, TURN = (2, 3, 1, 0), (2, 3, 0, 1), 4
NEAR = [[4 * q + k for k in NEAR_ORDER] for q in range(4)]
FAR = [[4 * q + k for q in FAR_ORDER] for k in range(4)]
LINE = [[(i - TURN) % TX for i in range(TX)]]
ROWS = 72
LANES = 128
GROUPS = 4
MAP = 33
VMEM = pl.BlockSpec(memory_space=pltpu.VMEM)
SMEM = pl.BlockSpec(memory_space=pltpu.SMEM)
PARAMS = pltpu.CompilerParams(vmem_limit_bytes=32 * 1024 * 1024)


def mm(a, b):
    return [
        a[3 * r] * b[c] + a[3 * r + 1] * b[3 + c] + a[3 * r + 2] * b[6 + c]
        for r in range(3)
        for c in range(3)
    ]


def mv(a, v):
    return [a[3 * r] * v[0] + a[3 * r + 1] * v[1] + a[3 * r + 2] * v[2] for r in range(3)]


def add(a, b):
    return [x + y for x, y in zip(a, b)]


def iota(shape, axis):
    return lax.broadcasted_iota(jnp.int32, shape, axis)


def swap_blocks(parts):
    block = iota(parts[0].shape, 1) // NZ
    for bit in (1, 2, 4):
        low = (block & bit) == 0
        fresh = list(parts)
        for i in range(8):
            if i & bit == 0:
                first, second = parts[i], parts[i | bit]
                fresh[i] = jnp.where(low, first, pltpu.roll(second, bit * NZ, 1))
                fresh[i | bit] = jnp.where(low, pltpu.roll(first, LANES - bit * NZ, 1), second)
        parts = fresh
    return parts


def halves(g):
    return [((g * LANES + h * 64 + TURN * 16) % 512, slice(h * 64, h * 64 + 64)) for h in range(2)]


def in_order(ref, g, first):
    return jnp.concatenate([ref[at : at + 64, first : first + LANES].astype(F32) for at, _ in halves(g)], axis=0)


def load_blocks(blocks, coef):
    for k in range(27):
        rows = blocks[k].astype(F32)
        for g in range(GROUPS):
            coef[pl.ds(g * 432 + k * CX, CX), :] = rows[:, g * LANES : (g + 1) * LANES]


def x_matrix(coef, x, first):
    return [coef[pl.ds((first + k) * CX + x, GROUPS, stride=432), :] for k in range(9)]


def depth(v, z):
    up = jnp.where(z < NZ - 1, pltpu.roll(v, LANES - 1, 1) - v, 0.0)
    down = jnp.where(z > 0, v - pltpu.roll(v, 1, 1), 0.0)
    return up - down


def prepare_x(*refs):
    inputs, (packed, base) = refs[0:7], refs[7:9]
    buffers, arrived = refs[9:16], refs[16]
    coef, fields, prefix, feats, pan = refs[17:]
    copies = [pltpu.make_async_copy(inputs[k], buffers[k], arrived.at[k]) for k in range(7)]
    for copy in copies:
        copy.start()
    pressure, exchange, blocks, labels, panels, tiles, counts = buffers
    copies[0].wait()
    copies[1].wait()
    for g in range(GROUPS):
        cut = slice(g * LANES, (g + 1) * LANES)
        for k in range(3):
            fields[pl.ds(g * 128 + k * CX, CX), :] = pressure[k, :, cut]
        for x in range(CX):
            fields[pl.ds(g * 128 + 64 + x * 2, 2), :] = exchange[x, :, cut]
    z = iota((GROUPS, LANES), 1) & (NZ - 1)
    for x in range(CX):
        field = [fields[pl.ds(k * CX + x, GROUPS, stride=128), :] for k in range(3)]
        rates = [fields[pl.ds(64 + x * 2 + k, GROUPS, stride=128), :] for k in range(2)]
        inflow = rates[0] * (field[0] - field[1])
        outflow = rates[1] * (field[1] - field[2])
        base[x * 3] = field[0] - inflow + 0.2 * depth(field[0], z)
        base[x * 3 + 1] = field[1] + inflow - outflow + 0.2 * depth(field[1], z)
        base[x * 3 + 2] = field[2] + outflow + 0.2 * depth(field[2], z)
    for g in range(GROUPS):
        feats[pl.ds(g * 256 + 96, 160), :] = jnp.zeros((160, LANES), F32)
    copies[2].wait()
    load_blocks(blocks, coef)
    copies[3].wait()
    where_from = labels[...]
    where_from = (where_from // (TY * 4)) * 4 + (where_from & 3)
    where_from = where_from.astype(F32)
    for g in range(GROUPS):
        feats[pl.ds(g * 256 + 96, CX), :] = where_from[:, g * LANES : (g + 1) * LANES]

    u = x_matrix(coef, 0, 18)
    for x in range(1, CX):
        for k in range(9):
            prefix[x * 9 + k] = u[k]
        if x < CX - 1:
            u = mm(u, x_matrix(coef, x, 18))
    c_map = mm(u, x_matrix(coef, CX - 1, 18))

    def put(row, value):
        feats[pl.ds(row, GROUPS, stride=256), :] = value

    s, w = None, None
    b, e = None, None
    for x in reversed(range(CX)):
        ux = [prefix[x * 9 + k] for k in range(9)] if x > 0 else None
        if x == CX - 1:
            w = ux
        else:
            p = x_matrix(coef, x + 1, 0)
            s = p if s is None else mm(s, p)
            w = mm(w, p)
            if x > 0:
                w = add(w, ux)
            else:
                for k in (0, 4, 8):
                    w[k] = w[k] + 1.0
        gain = x_matrix(coef, x, 9)
        r = [base[x * 3 + k] for k in range(3)]
        column = [gain[0], gain[3], gain[6]]
        pushed = mv(gain, r)
        kb = column if s is None else mv(s, column)
        ke = mv(w, column)
        sb = pushed if s is None else mv(s, pushed)
        se = mv(w, pushed)
        b = sb if b is None else add(b, sb)
        e = se if e is None else add(e, se)
        for k in range(3):
            put(k * CX + x, kb[k])
            put((3 + k) * CX + x, ke[k])
    p = x_matrix(coef, 0, 0)
    values = mm(s, p) + c_map + mm(w, p) + b + e
    for k in range(MAP):
        high = values[k].astype(BF16).astype(F32)
        put(128 + k, high)
        put(128 + MAP + k, values[k] - high)

    for k in range(4, 7):
        copies[k].wait()
    for k in range(4):
        pan[pl.ds(k * 4, 4), :] = panels[k].astype(F32)
    row, column = iota((16, 4), 0), iota((16, 4), 1)
    listed = jnp.concatenate([jnp.broadcast_to(tiles[k : k + 1, :], (4, 4)) for k in range(4)], axis=0)
    limits = jnp.broadcast_to(counts[...], (16, 4))
    listed = jnp.sum(jnp.where(column == (row & 3), listed.astype(F32), 0.0), axis=1, keepdims=True)
    limits = jnp.sum(jnp.where(column == row // 4, limits.astype(F32), 0.0), axis=1, keepdims=True)
    routes = jnp.where((row[:, 0:1] & 3).astype(F32) < limits, listed, -1.0)
    routes = jnp.broadcast_to(routes, (16, LANES))
    routes = jnp.concatenate([routes] * 8, axis=0)
    lane = iota((LANES, LANES), 1)
    for g in range(GROUPS):
        slab = pan[:, g * LANES : (g + 1) * LANES]
        pieces = [pltpu.roll(slab, (112 - i * NZ) % LANES, 1) if i < 7 else slab for i in range(8)]
        first = feats[pl.ds(g * 256, LANES), :].T
        first = jnp.where(lane >= 112, jnp.concatenate(pieces, axis=0), first)
        for at, part in halves(g):
            packed[at : at + 64, 0:LANES] = first[part, :].astype(BF16)
        second = feats[pl.ds(g * 256 + LANES, LANES), :].T
        second = jnp.where(lane == 72, routes, second)
        for at, part in halves(g):
            packed[at : at + 64, LANES : 2 * LANES] = second[part, :].astype(BF16)


def solve_x(received, answer, low, high, spread, target, out):
    for g in range(GROUPS):
        rows = slice(g * LANES, (g + 1) * LANES)
        low[rows, :] = in_order(received, g, 0).T
        high[rows, :] = in_order(received, g, LANES).T
    r_id, c_id = iota((LANES, LANES), 0), iota((LANES, LANES), 1)
    lane = iota((512, LANES), 1)
    copy_panel = ((r_id >= 112) & ((r_id - 112) == (c_id & (NZ - 1)))).astype(F32).astype(BF16)
    copy_route = (r_id == 72).astype(F32).astype(BF16)
    panel_part = jnp.concatenate([in_order(received, g, 0) for g in range(GROUPS)], axis=0)
    panel_part = jnp.where(lane >= 112, panel_part, 0.0).astype(BF16)
    route_part = jnp.concatenate([in_order(received, g, LANES) for g in range(GROUPS)], axis=0)
    route_part = jnp.where(lane == 72, route_part, 0.0).astype(BF16)
    spread[...] = jnp.dot(panel_part, copy_panel, preferred_element_type=F32)
    target[...] = jnp.dot(route_part, copy_route, preferred_element_type=F32)
    tile_lane = (c_id // NZ).astype(F32)
    for g in range(GROUPS):
        table = None
        for j in range(4):
            hit = target[pl.ds(j, LANES, stride=4), :] == tile_lane + 8.0 * g
            part = jnp.where(hit, spread[pl.ds(j, LANES, stride=4), :], 0.0)
            table = part if table is None else table + part
        position = low[pl.ds(g * LANES + 96, CX), :].astype(jnp.int32)
        found = []
        for half in range(2):
            place = position[half * 8 : half * 8 + 8, :]
            inner, outer = place & 7, place // 8
            picked = jnp.zeros((8, LANES), F32)
            for o in range(16):
                chosen = jnp.take_along_axis(table[o * 8 : o * 8 + 8, :], inner, axis=0)
                picked = jnp.where(outer == o, chosen, picked)
            found.append(picked)
        source = jnp.concatenate(found, axis=0)
        out[pl.ds(g * LANES + 24, CX), :] = source
        for k in range(6):
            response = low[pl.ds(g * LANES + k * CX, CX), :]
            extra = jnp.sum(response * source, axis=0, keepdims=True)
            at = pl.ds(g * LANES + 27 + k, 1)
            high[at, :] = high[at, :] + extra

    def value(k):
        return high[pl.ds(k, 8, stride=LANES), :] + high[pl.ds(MAP + k, 8, stride=LANES), :]

    lanes8 = iota((8, LANES), 1)
    tile = iota((8, LANES), 0) * 8 + lanes8 // NZ

    def before(v, d, fill):
        if d < 8:
            turned = pltpu.roll(v, d * NZ, 1)
            moved = jnp.where(lanes8 >= d * NZ, turned, pltpu.roll(turned, 1, 0))
        else:
            moved = pltpu.roll(v, d // 8, 0)
        return jnp.where(tile >= d, moved, fill)

    def after(v, d, fill):
        if d < 8:
            turned = pltpu.roll(v, LANES - d * NZ, 1)
            moved = jnp.where(lanes8 < LANES - d * NZ, turned, pltpu.roll(turned, 7, 0))
        else:
            moved = pltpu.roll(v, 8 - d // 8, 0)
        return jnp.where(tile + d < TX, moved, fill)

    def scan(matrix, vector, shift):
        for d in (1, 2, 4, 8, 16):
            vector_now = add(mv(matrix, [shift(v, d, 0.0) for v in vector]), vector)
            if d < 16:
                matrix = mm(matrix, [shift(m, d, 1.0 if k in (0, 4, 8) else 0.0) for k, m in enumerate(matrix)])
            vector = vector_now
        return [shift(v, 1, 0.0) for v in vector]

    enter = scan([value(k) for k in range(9)], [value(27 + k) for k in range(3)], before)
    pushed = add(mv([value(18 + k) for k in range(9)], enter), [value(30 + k) for k in range(3)])
    finish = scan([value(9 + k) for k in range(9)], pushed, after)
    for k, v in enumerate(enter + finish):
        for piece in range(3):
            part = v.astype(BF16).astype(F32)
            out[pl.ds(piece * 6 + k, 8, stride=LANES), :] = part
            v = v - part
    for g in range(GROUPS):
        rows = slice(g * LANES, (g + 1) * LANES)
        turned_out = out[rows, :].T.astype(BF16)
        for at, part in halves(g):
            answer[at : at + 64, :] = turned_out[part, :]


def prepare_y(place, blocks, turned, parts, whole, spot, plain, coef):
    spot[...] = jnp.full((8, LANES), place[0], jnp.int32)
    load_blocks(blocks, plain)
    for half in range(2):
        for g in range(GROUPS):
            rows = swap_blocks([plain[pl.ds(g * 432 + half * 8 + i, 27, stride=CX), :] for i in range(8)])
            for y in range(8):
                coef[pl.ds((g * 2 + half) * 256 + y * 32, 27), :] = rows[y]
    phi, u, d_map = None, None, None
    for y in range(8):
        block = [coef[pl.ds(y * 32 + k, 8, stride=256), :] for k in range(27)]
        for k in range(27):
            turned[y * 27 + k] = block[k]
        phi = block[0:9] if y == 0 else mm(block[0:9], phi)
        d_map = phi if y == 0 else add(d_map, mm(u, phi))
        u = block[18:27] if y == 0 else mm(u, block[18:27])
    for k, v in enumerate(phi + u + d_map):
        parts[pl.ds(k * 8, 8), :] = v
    a, c, d = [quarter(parts, 0, 9 * k, 9) for k in range(3)]
    for l in range(1, GROUPS):
        a_l, c_l, d_l = [quarter(parts, l, 9 * k, 9) for k in range(3)]
        d = add(mm(mm(c, d_l), a), d)
        a = mm(a_l, a)
        c = mm(c, c_l)
    for k, v in enumerate(a + c + d):
        whole[pl.ds(k * 2, 2), :] = v
    whole[pl.ds(54, 2), :] = jnp.zeros((2, LANES), F32)


def quarter(ref, l, first, count):
    return [ref[pl.ds((first + k) * 8 + l * 2, 2), :] for k in range(count)]


def finish_x(received, base, blocks, turned, parts, whole, sent, values, ends, coef, low, stage, lined):
    load_blocks(blocks, coef)
    for g in range(GROUPS):
        rows = slice(g * LANES, (g + 1) * LANES)
        low[rows, :] = in_order(received, g, 0).T

    def entry(k):
        rows = [low[pl.ds(piece * 6 + k, GROUPS, stride=LANES), :] for piece in range(3)]
        return rows[0] + rows[1] + rows[2]

    f = [entry(k) for k in range(3)]
    a = [entry(3 + k) for k in range(3)]
    forward = []
    for x in range(CX):
        source = low[pl.ds(24 + x, GROUPS, stride=LANES), :]
        r = [base[x * 3] + source, base[x * 3 + 1], base[x * 3 + 2]]
        f = add(mv(x_matrix(coef, x, 0), f), mv(x_matrix(coef, x, 9), r))
        forward.append(f)
    for x in reversed(range(CX)):
        a = add(mv(x_matrix(coef, x, 18), a), forward[x])
        for k in range(3):
            stage[pl.ds(x * 16 + k * 4, 4), :] = a[k]
    for half in range(2):
        rows = swap_blocks([stage[pl.ds((half * 8 + i) * 16, 16), :] for i in range(8)])
        for y in range(8):
            for k in range(3):
                lined[pl.ds(half * 24 + y * 3 + k, 4, stride=48), :] = rows[y][k * 4 : k * 4 + 4, :]
    f, forward = None, []
    for y in range(8):
        r = [lined[pl.ds(y * 3 + k, 8, stride=24), :] for k in range(3)]
        pushed = mv([turned[y * 27 + 9 + k] for k in range(9)], r)
        for k in range(3):
            values[y * 3 + k] = pushed[k]
        f = pushed if f is None else add(mv([turned[y * 27 + k] for k in range(9)], f), pushed)
        forward.append(f)
    a = None
    for y in reversed(range(8)):
        a = forward[y] if a is None else add(mv([turned[y * 27 + 18 + k] for k in range(9)], a), forward[y])
    for k, v in enumerate(forward[7] + a):
        ends[pl.ds(k * 8, 8), :] = v
    enter, f = [], None
    for l in range(GROUPS):
        enter.append(f)
        b_l = quarter(ends, l, 0, 3)
        f = b_l if f is None else add(mv(quarter(parts, l, 0, 9), f), b_l)
    a = None
    for l in reversed(range(GROUPS)):
        now = quarter(ends, l, 3, 3)
        if enter[l] is not None:
            now = add(now, mv(quarter(parts, l, 18, 9), enter[l]))
        a = now if a is None else add(mv(quarter(parts, l, 9, 9), a), now)
    put_map(sent, [whole[pl.ds(k * 2, 2), :] for k in range(27)] + f + a)


def put_map(sent, values):
    for k, v in enumerate(values):
        sent[pl.ds(k * 2, 2), :] = v
    sent[pl.ds(66, 6), :] = jnp.zeros((6, LANES), F32)
    for i in range(1, 4):
        sent[pl.ds(i * ROWS, ROWS), :] = sent[pl.ds(0, ROWS), :]


def get_map(ref, order, i):
    i = order.index(i)
    v = [ref[pl.ds(i * ROWS + k * 2, 2), :] for k in range(MAP)]
    return v[0:9], v[9:18], v[18:27], v[27:30], v[30:33]


def join_y(received, sent):
    a, c, d, b, e = get_map(received, NEAR_ORDER, 0)
    for i in range(1, 4):
        a1, c1, d1, b1, e1 = get_map(received, NEAR_ORDER, i)
        e = add(mv(c, add(mv(d1, b), e1)), e)
        d = add(mm(c, mm(d1, a)), d)
        b = add(mv(a1, b), b1)
        a = mm(a1, a)
        c = mm(c, c1)
    put_map(sent, a + c + d + b + e)


def narrow(received, order, mine, enter, finish):
    maps = [get_map(received, order, i) for i in range(4)]
    fs = [enter]
    for i in range(3):
        fs.append(add(mv(maps[i][0], fs[i]), maps[i][3]))
    ends = [None, None, None, finish]
    for i in (3, 2, 1):
        _, c, d, _, e = maps[i]
        ends[i - 1] = add(add(mv(c, ends[i]), mv(d, fs[i])), e)
    enter, finish = fs[0], ends[0]
    for i in range(1, 4):
        enter = [jnp.where(mine == i, n, o) for n, o in zip(fs[i], enter)]
        finish = [jnp.where(mine == i, n, o) for n, o in zip(ends[i], finish)]
    return enter, finish


def finish_y(spot, near, far, values, ends, turned, parts, result, edge):
    me = spot[0:2, :]
    zero = [jnp.zeros((2, LANES), F32) for _ in range(3)]
    enter, finish = narrow(far, FAR_ORDER, me // 4, zero, zero)
    enter, finish = narrow(near, NEAR_ORDER, me % 4, enter, finish)
    f = enter
    inside = []
    for l in range(GROUPS):
        inside.append(f)
        for k in range(3):
            edge[pl.ds(k * 8 + l * 2, 2), :] = f[k]
        if l < GROUPS - 1:
            f = add(mv(quarter(parts, l, 0, 9), f), quarter(ends, l, 0, 3))
    a = finish
    for l in reversed(range(GROUPS)):
        for k in range(3):
            edge[pl.ds(24 + k * 8 + l * 2, 2), :] = a[k]
        if l > 0:
            a = add(
                add(mv(quarter(parts, l, 9, 9), a), mv(quarter(parts, l, 18, 9), inside[l])),
                quarter(ends, l, 3, 3),
            )
    f = [edge[pl.ds(k * 8, 8), :] for k in range(3)]
    a = [edge[pl.ds(24 + k * 8, 8), :] for k in range(3)]
    forward = []
    for y in range(8):
        f = add(mv([turned[y * 27 + k] for k in range(9)], f), [values[y * 3 + k] for k in range(3)])
        forward.append(f)
    solved = [None] * 8
    for y in reversed(range(8)):
        a = add(mv([turned[y * 27 + 18 + k] for k in range(9)], a), forward[y])
        solved[y] = a
    for k in range(3):
        rows = swap_blocks([solved[y][k] for y in range(8)])
        for x in range(8):
            for g in range(GROUPS):
                for half in range(2):
                    at = g * 2 + half
                    result[k, pl.ds(half * 8 + x, 1), g * LANES : (g + 1) * LANES] = rows[x][at : at + 1, :]


def body(pressure, exchange_rates, x_blocks, y_blocks, panels, outlet_tiles, outlet_counts, labels):
    shape = jax.ShapeDtypeStruct
    pressure, x_blocks, y_blocks = [jnp.transpose(v, (1, 0, 2)) for v in (pressure, x_blocks, y_blocks)]
    inputs = (pressure, exchange_rates, x_blocks, labels, panels, outlet_tiles, outlet_counts.reshape(1, 4))
    place = lax.axis_index("gy").astype(jnp.int32).reshape(1)
    packed, base = pl.pallas_call(
        prepare_x,
        out_shape=(shape((512, 256), BF16), shape((CX * 3, GROUPS, LANES), F32)),
        in_specs=[pl.BlockSpec(memory_space=pltpu.HBM)] * 7,
        out_specs=(VMEM,) * 2,
        scratch_shapes=[pltpu.VMEM(v.shape, v.dtype) for v in inputs]
        + [
            pltpu.SemaphoreType.DMA((7,)),
            pltpu.VMEM((1728, LANES), F32),
            pltpu.VMEM((512, LANES), F32),
            pltpu.VMEM((CX * 9, GROUPS, LANES), F32),
            pltpu.VMEM((1024, LANES), F32),
            pltpu.VMEM((16, 512), F32),
        ],
        name="prepare_x",
    )(*inputs)
    received = lax.all_to_all(packed, "gx", split_axis=0, concat_axis=0, tiled=True, axis_index_groups=LINE)
    turned, parts, whole, spot = pl.pallas_call(
        prepare_y,
        out_shape=(
            shape((8 * 27, 8, LANES), F32),
            shape((27 * 8, LANES), F32),
            shape((56, LANES), F32),
            shape((8, LANES), jnp.int32),
        ),
        in_specs=[SMEM, VMEM],
        out_specs=(VMEM,) * 4,
        scratch_shapes=[pltpu.VMEM((1728, LANES), F32), pltpu.VMEM((2048, LANES), F32)],
        compiler_params=PARAMS,
        name="prepare_y",
    )(place, y_blocks)
    received, whole = lax.optimization_barrier((received, whole))
    answer = pl.pallas_call(
        solve_x,
        out_shape=shape((512, LANES), BF16),
        in_specs=[VMEM],
        out_specs=VMEM,
        scratch_shapes=[
            pltpu.VMEM((512, LANES), F32),
            pltpu.VMEM((1024, LANES), F32),
            pltpu.VMEM((512, LANES), F32),
            pltpu.VMEM((512, LANES), F32),
            pltpu.VMEM((1024, LANES), F32),
        ],
        compiler_params=PARAMS,
        name="solve_x",
    )(received)
    entries = lax.all_to_all(answer, "gx", split_axis=0, concat_axis=0, tiled=True, axis_index_groups=LINE)
    sent, values, ends = pl.pallas_call(
        finish_x,
        out_shape=(
            shape((4 * ROWS, LANES), F32),
            shape((24, 8, LANES), F32),
            shape((48, LANES), F32),
        ),
        in_specs=[VMEM] * 6,
        out_specs=(VMEM,) * 3,
        scratch_shapes=[
            pltpu.VMEM((1728, LANES), F32),
            pltpu.VMEM((512, LANES), F32),
            pltpu.VMEM((256, LANES), F32),
            pltpu.VMEM((192, LANES), F32),
        ],
        compiler_params=PARAMS,
        name="finish_x",
    )(entries, base, x_blocks, turned, parts, whole)
    near = lax.all_to_all(sent, "gy", split_axis=0, concat_axis=0, tiled=True, axis_index_groups=NEAR)
    joined = pl.pallas_call(
        join_y,
        out_shape=shape((4 * ROWS, LANES), F32),
        in_specs=[VMEM],
        out_specs=VMEM,
        compiler_params=PARAMS,
        name="join_y",
    )(near)
    far = lax.all_to_all(joined, "gy", split_axis=0, concat_axis=0, tiled=True, axis_index_groups=FAR)
    result = pl.pallas_call(
        finish_y,
        out_shape=shape((3, CX, 512), F32),
        in_specs=[VMEM] * 7,
        out_specs=VMEM,
        scratch_shapes=[pltpu.VMEM((48, LANES), F32)],
        compiler_params=PARAMS,
        name="finish_y",
    )(spot, near, far, values, ends, turned, parts)
    return jnp.transpose(result, (1, 0, 2))


def solution(mesh):
    in_specs = (
        P("gx", None, "gy"),
        P("gx", None, "gy"),
        P("gx", None, "gy"),
        P("gx", None, "gy"),
        P(("gx", "gy"), None, None),
        P(("gx", "gy"), None),
        P(("gx", "gy")),
        P("gx", "gy"),
    )
    out_specs = P("gx", None, "gy")
    return jax.shard_map(body, mesh=mesh, in_specs=in_specs, out_specs=out_specs, check_vma=False)
```

```python
import jax
import jax.numpy as jnp
from jax import lax
from jax.experimental import pallas as pl
from jax.experimental.pallas import tpu as pltpu
from jax.sharding import PartitionSpec as P

F32 = jnp.float32
BF16 = jnp.bfloat16
CX, CY, NZ = 16, 32, 16
TX, TY = 32, 16
NEAR_ORDER, FAR_ORDER, TURN = (1, 2, 3, 0), (2, 3, 0, 1), 4
NEAR = [[4 * q + k for k in NEAR_ORDER] for q in range(4)]
FAR = [[4 * q + k for q in FAR_ORDER] for k in range(4)]
LINE = [[(i - TURN) % TX for i in range(TX)]]
ROWS = 72
LANES = 128
GROUPS = 4
MAP = 33
VMEM = pl.BlockSpec(memory_space=pltpu.VMEM)
SMEM = pl.BlockSpec(memory_space=pltpu.SMEM)
PARAMS = pltpu.CompilerParams(vmem_limit_bytes=32 * 1024 * 1024)


def mm(a, b):
    return [
        a[3 * r] * b[c] + a[3 * r + 1] * b[3 + c] + a[3 * r + 2] * b[6 + c]
        for r in range(3)
        for c in range(3)
    ]


def mv(a, v):
    return [a[3 * r] * v[0] + a[3 * r + 1] * v[1] + a[3 * r + 2] * v[2] for r in range(3)]


def add(a, b):
    return [x + y for x, y in zip(a, b)]


def iota(shape, axis):
    return lax.broadcasted_iota(jnp.int32, shape, axis)


def swap_blocks(parts):
    block = iota(parts[0].shape, 1) // NZ
    for bit in (1, 2, 4):
        low = (block & bit) == 0
        fresh = list(parts)
        for i in range(8):
            if i & bit == 0:
                first, second = parts[i], parts[i | bit]
                fresh[i] = jnp.where(low, first, pltpu.roll(second, bit * NZ, 1))
                fresh[i | bit] = jnp.where(low, pltpu.roll(first, LANES - bit * NZ, 1), second)
        parts = fresh
    return parts


def halves(g):
    return [((g * LANES + h * 64 + TURN * 16) % 512, slice(h * 64, h * 64 + 64)) for h in range(2)]


def in_order(ref, g, first):
    return jnp.concatenate([ref[at : at + 64, first : first + LANES].astype(F32) for at, _ in halves(g)], axis=0)


def load_blocks(blocks, coef):
    for k in range(27):
        rows = blocks[k].astype(F32)
        for g in range(GROUPS):
            coef[pl.ds(g * 432 + k * CX, CX), :] = rows[:, g * LANES : (g + 1) * LANES]


def x_matrix(coef, x, first):
    return [coef[pl.ds((first + k) * CX + x, GROUPS, stride=432), :] for k in range(9)]


def depth(v, z):
    up = jnp.where(z < NZ - 1, pltpu.roll(v, LANES - 1, 1) - v, 0.0)
    down = jnp.where(z > 0, v - pltpu.roll(v, 1, 1), 0.0)
    return up - down


def prepare_x(*refs):
    inputs, (packed, base) = refs[0:7], refs[7:9]
    buffers, arrived = refs[9:16], refs[16]
    coef, fields, prefix, feats, pan = refs[17:]
    copies = [pltpu.make_async_copy(inputs[k], buffers[k], arrived.at[k]) for k in range(7)]
    for copy in copies:
        copy.start()
    pressure, exchange, blocks, labels, panels, tiles, counts = buffers
    copies[0].wait()
    copies[1].wait()
    for g in range(GROUPS):
        cut = slice(g * LANES, (g + 1) * LANES)
        for k in range(3):
            fields[pl.ds(g * 128 + k * CX, CX), :] = pressure[k, :, cut]
        for x in range(CX):
            fields[pl.ds(g * 128 + 64 + x * 2, 2), :] = exchange[x, :, cut]
    z = iota((GROUPS, LANES), 1) & (NZ - 1)
    for x in range(CX):
        field = [fields[pl.ds(k * CX + x, GROUPS, stride=128), :] for k in range(3)]
        rates = [fields[pl.ds(64 + x * 2 + k, GROUPS, stride=128), :] for k in range(2)]
        inflow = rates[0] * (field[0] - field[1])
        outflow = rates[1] * (field[1] - field[2])
        base[x * 3] = field[0] - inflow + 0.2 * depth(field[0], z)
        base[x * 3 + 1] = field[1] + inflow - outflow + 0.2 * depth(field[1], z)
        base[x * 3 + 2] = field[2] + outflow + 0.2 * depth(field[2], z)
    for g in range(GROUPS):
        feats[pl.ds(g * 256 + 192, 64), :] = jnp.zeros((64, LANES), F32)
    copies[2].wait()
    load_blocks(blocks, coef)
    copies[3].wait()
    where_from = labels[...]
    where_from = (where_from // (TY * 4)) * 4 + (where_from & 3)
    where_from = where_from.astype(F32)
    for g in range(GROUPS):
        feats[pl.ds(g * 256 + 96, CX), :] = where_from[:, g * LANES : (g + 1) * LANES]

    u = x_matrix(coef, 0, 18)
    for x in range(1, CX):
        for k in range(9):
            prefix[x * 9 + k] = u[k]
        if x < CX - 1:
            u = mm(u, x_matrix(coef, x, 18))
    c_map = mm(u, x_matrix(coef, CX - 1, 18))

    def put(row, value):
        feats[pl.ds(row, GROUPS, stride=256), :] = value

    s, w = None, None
    b, e = None, None
    for x in reversed(range(CX)):
        ux = [prefix[x * 9 + k] for k in range(9)] if x > 0 else None
        if x == CX - 1:
            w = ux
        else:
            p = x_matrix(coef, x + 1, 0)
            s = p if s is None else mm(s, p)
            w = mm(w, p)
            if x > 0:
                w = add(w, ux)
            else:
                for k in (0, 4, 8):
                    w[k] = w[k] + 1.0
        gain = x_matrix(coef, x, 9)
        r = [base[x * 3 + k] for k in range(3)]
        column = [gain[0], gain[3], gain[6]]
        pushed = mv(gain, r)
        kb = column if s is None else mv(s, column)
        ke = mv(w, column)
        sb = pushed if s is None else mv(s, pushed)
        se = mv(w, pushed)
        b = sb if b is None else add(b, sb)
        e = se if e is None else add(e, se)
        for k in range(3):
            put(k * CX + x, kb[k])
            put((3 + k) * CX + x, ke[k])
    p = x_matrix(coef, 0, 0)
    values = mm(s, p) + c_map + mm(w, p) + b + e
    for k in range(MAP):
        high = values[k].astype(BF16).astype(F32)
        put(128 + k, high)
        put(128 + MAP + k, values[k] - high)

    for k in range(4, 7):
        copies[k].wait()
    for k in range(4):
        pan[pl.ds(k * 4, 4), :] = panels[k].astype(F32)
    row, column = iota((16, 4), 0), iota((16, 4), 1)
    listed = jnp.concatenate([jnp.broadcast_to(tiles[k : k + 1, :], (4, 4)) for k in range(4)], axis=0)
    limits = jnp.broadcast_to(counts[...], (16, 4))
    listed = jnp.sum(jnp.where(column == (row & 3), listed.astype(F32), 0.0), axis=1, keepdims=True)
    limits = jnp.sum(jnp.where(column == row // 4, limits.astype(F32), 0.0), axis=1, keepdims=True)
    routes = jnp.where((row[:, 0:1] & 3).astype(F32) < limits, listed, -1.0)
    routes = jnp.broadcast_to(routes, (16, LANES))
    routes = jnp.concatenate([routes] * 8, axis=0)
    lane = iota((LANES, LANES), 1)
    for g in range(GROUPS):
        slab = pan[:, g * LANES : (g + 1) * LANES]
        pieces = [pltpu.roll(slab, (112 - i * NZ) % LANES, 1) if i < 7 else slab for i in range(8)]
        first = feats[pl.ds(g * 256, LANES), :].T
        first = jnp.where(lane >= 112, jnp.concatenate(pieces, axis=0), first)
        for at, part in halves(g):
            packed[at : at + 64, 0:LANES] = first[part, :].astype(BF16)
        second = feats[pl.ds(g * 256 + LANES, LANES), :].T
        second = jnp.where(lane == 72, routes, second)
        for at, part in halves(g):
            packed[at : at + 64, LANES : 2 * LANES] = second[part, :].astype(BF16)


def solve_x(received, answer, low, high, spread, target, out):
    for g in range(GROUPS):
        rows = slice(g * LANES, (g + 1) * LANES)
        low[rows, :] = in_order(received, g, 0).T
        high[rows, :] = in_order(received, g, LANES).T
    r_id, c_id = iota((LANES, LANES), 0), iota((LANES, LANES), 1)
    lane = iota((512, LANES), 1)
    copy_panel = ((r_id >= 112) & ((r_id - 112) == (c_id & (NZ - 1)))).astype(F32).astype(BF16)
    copy_route = (r_id == 72).astype(F32).astype(BF16)
    panel_part = jnp.concatenate([in_order(received, g, 0) for g in range(GROUPS)], axis=0)
    panel_part = jnp.where(lane >= 112, panel_part, 0.0).astype(BF16)
    route_part = jnp.concatenate([in_order(received, g, LANES) for g in range(GROUPS)], axis=0)
    route_part = jnp.where(lane == 72, route_part, 0.0).astype(BF16)
    spread[...] = jnp.dot(panel_part, copy_panel, preferred_element_type=F32)
    target[...] = jnp.dot(route_part, copy_route, preferred_element_type=F32)
    tile_lane = (c_id // NZ).astype(F32)
    for g in range(GROUPS):
        table = None
        for j in range(4):
            hit = target[pl.ds(j, LANES, stride=4), :] == tile_lane + 8.0 * g
            part = jnp.where(hit, spread[pl.ds(j, LANES, stride=4), :], 0.0)
            table = part if table is None else table + part
        position = low[pl.ds(g * LANES + 96, CX), :].astype(jnp.int32)
        found = []
        for half in range(2):
            place = position[half * 8 : half * 8 + 8, :]
            inner, outer = place & 7, place // 8
            picked = jnp.zeros((8, LANES), F32)
            for o in range(16):
                chosen = jnp.take_along_axis(table[o * 8 : o * 8 + 8, :], inner, axis=0)
                picked = jnp.where(outer == o, chosen, picked)
            found.append(picked)
        source = jnp.concatenate(found, axis=0)
        out[pl.ds(g * LANES + 24, CX), :] = source
        for k in range(6):
            response = low[pl.ds(g * LANES + k * CX, CX), :]
            extra = jnp.sum(response * source, axis=0, keepdims=True)
            at = pl.ds(g * LANES + 27 + k, 1)
            high[at, :] = high[at, :] + extra

    def value(k):
        return high[pl.ds(k, 8, stride=LANES), :] + high[pl.ds(MAP + k, 8, stride=LANES), :]

    lanes8 = iota((8, LANES), 1)
    tile = iota((8, LANES), 0) * 8 + lanes8 // NZ

    def before(v, d, fill):
        if d < 8:
            turned = pltpu.roll(v, d * NZ, 1)
            moved = jnp.where(lanes8 >= d * NZ, turned, pltpu.roll(turned, 1, 0))
        else:
            moved = pltpu.roll(v, d // 8, 0)
        return jnp.where(tile >= d, moved, fill)

    def after(v, d, fill):
        if d < 8:
            turned = pltpu.roll(v, LANES - d * NZ, 1)
            moved = jnp.where(lanes8 < LANES - d * NZ, turned, pltpu.roll(turned, 7, 0))
        else:
            moved = pltpu.roll(v, 8 - d // 8, 0)
        return jnp.where(tile + d < TX, moved, fill)

    def scan(matrix, vector, shift):
        for d in (1, 2, 4, 8, 16):
            vector_now = add(mv(matrix, [shift(v, d, 0.0) for v in vector]), vector)
            if d < 16:
                matrix = mm(matrix, [shift(m, d, 1.0 if k in (0, 4, 8) else 0.0) for k, m in enumerate(matrix)])
            vector = vector_now
        return [shift(v, 1, 0.0) for v in vector]

    enter = scan([value(k) for k in range(9)], [value(27 + k) for k in range(3)], before)
    pushed = add(mv([value(18 + k) for k in range(9)], enter), [value(30 + k) for k in range(3)])
    finish = scan([value(9 + k) for k in range(9)], pushed, after)
    for k, v in enumerate(enter + finish):
        for piece in range(3):
            part = v.astype(BF16).astype(F32)
            out[pl.ds(piece * 6 + k, 8, stride=LANES), :] = part
            v = v - part
    for g in range(GROUPS):
        rows = slice(g * LANES, (g + 1) * LANES)
        turned_out = out[rows, :].T.astype(BF16)
        for at, part in halves(g):
            answer[at : at + 64, :] = turned_out[part, :]


def prepare_y(place, blocks, turned, parts, whole, spot, plain, coef):
    spot[...] = jnp.full((8, LANES), place[0], jnp.int32)
    load_blocks(blocks, plain)
    for half in range(2):
        for g in range(GROUPS):
            rows = swap_blocks([plain[pl.ds(g * 432 + half * 8 + i, 27, stride=CX), :] for i in range(8)])
            for y in range(8):
                coef[pl.ds((g * 2 + half) * 256 + y * 32, 27), :] = rows[y]
    phi, u, d_map = None, None, None
    for y in range(8):
        block = [coef[pl.ds(y * 32 + k, 8, stride=256), :] for k in range(27)]
        for k in range(27):
            turned[y * 27 + k] = block[k]
        phi = block[0:9] if y == 0 else mm(block[0:9], phi)
        d_map = phi if y == 0 else add(d_map, mm(u, phi))
        u = block[18:27] if y == 0 else mm(u, block[18:27])
    for k, v in enumerate(phi + u + d_map):
        parts[pl.ds(k * 8, 8), :] = v
    a, c, d = [quarter(parts, 0, 9 * k, 9) for k in range(3)]
    for l in range(1, GROUPS):
        a_l, c_l, d_l = [quarter(parts, l, 9 * k, 9) for k in range(3)]
        d = add(mm(mm(c, d_l), a), d)
        a = mm(a_l, a)
        c = mm(c, c_l)
    for k, v in enumerate(a + c + d):
        whole[pl.ds(k * 2, 2), :] = v
    whole[pl.ds(54, 2), :] = jnp.zeros((2, LANES), F32)


def quarter(ref, l, first, count):
    return [ref[pl.ds((first + k) * 8 + l * 2, 2), :] for k in range(count)]


def finish_x(received, base, blocks, turned, parts, whole, sent, values, ends, coef, low, stage, lined):
    load_blocks(blocks, coef)
    for g in range(GROUPS):
        rows = slice(g * LANES, (g + 1) * LANES)
        low[rows, :] = in_order(received, g, 0).T

    def entry(k):
        rows = [low[pl.ds(piece * 6 + k, GROUPS, stride=LANES), :] for piece in range(3)]
        return rows[0] + rows[1] + rows[2]

    f = [entry(k) for k in range(3)]
    a = [entry(3 + k) for k in range(3)]
    forward = []
    for x in range(CX):
        source = low[pl.ds(24 + x, GROUPS, stride=LANES), :]
        r = [base[x * 3] + source, base[x * 3 + 1], base[x * 3 + 2]]
        f = add(mv(x_matrix(coef, x, 0), f), mv(x_matrix(coef, x, 9), r))
        forward.append(f)
    for x in reversed(range(CX)):
        a = add(mv(x_matrix(coef, x, 18), a), forward[x])
        for k in range(3):
            stage[pl.ds(x * 16 + k * 4, 4), :] = a[k]
    for half in range(2):
        rows = swap_blocks([stage[pl.ds((half * 8 + i) * 16, 16), :] for i in range(8)])
        for y in range(8):
            for k in range(3):
                lined[pl.ds(half * 24 + y * 3 + k, 4, stride=48), :] = rows[y][k * 4 : k * 4 + 4, :]
    f, forward = None, []
    for y in range(8):
        r = [lined[pl.ds(y * 3 + k, 8, stride=24), :] for k in range(3)]
        pushed = mv([turned[y * 27 + 9 + k] for k in range(9)], r)
        for k in range(3):
            values[y * 3 + k] = pushed[k]
        f = pushed if f is None else add(mv([turned[y * 27 + k] for k in range(9)], f), pushed)
        forward.append(f)
    a = None
    for y in reversed(range(8)):
        a = forward[y] if a is None else add(mv([turned[y * 27 + 18 + k] for k in range(9)], a), forward[y])
    for k, v in enumerate(forward[7] + a):
        ends[pl.ds(k * 8, 8), :] = v
    enter, f = [], None
    for l in range(GROUPS):
        enter.append(f)
        b_l = quarter(ends, l, 0, 3)
        f = b_l if f is None else add(mv(quarter(parts, l, 0, 9), f), b_l)
    a = None
    for l in reversed(range(GROUPS)):
        now = quarter(ends, l, 3, 3)
        if enter[l] is not None:
            now = add(now, mv(quarter(parts, l, 18, 9), enter[l]))
        a = now if a is None else add(mv(quarter(parts, l, 9, 9), a), now)
    put_map(sent, [whole[pl.ds(k * 2, 2), :] for k in range(27)] + f + a)


def put_map(sent, values):
    for k, v in enumerate(values):
        sent[pl.ds(k * 2, 2), :] = v
    sent[pl.ds(66, 6), :] = jnp.zeros((6, LANES), F32)
    for i in range(1, 4):
        sent[pl.ds(i * ROWS, ROWS), :] = sent[pl.ds(0, ROWS), :]


def get_map(ref, order, i):
    i = order.index(i)
    v = [ref[pl.ds(i * ROWS + k * 2, 2), :] for k in range(MAP)]
    return v[0:9], v[9:18], v[18:27], v[27:30], v[30:33]


def join_y(received, sent):
    a, c, d, b, e = get_map(received, NEAR_ORDER, 0)
    for i in range(1, 4):
        a1, c1, d1, b1, e1 = get_map(received, NEAR_ORDER, i)
        e = add(mv(c, add(mv(d1, b), e1)), e)
        d = add(mm(c, mm(d1, a)), d)
        b = add(mv(a1, b), b1)
        a = mm(a1, a)
        c = mm(c, c1)
    put_map(sent, a + c + d + b + e)


def narrow(received, order, mine, enter, finish):
    maps = [get_map(received, order, i) for i in range(4)]
    fs = [enter]
    for i in range(3):
        fs.append(add(mv(maps[i][0], fs[i]), maps[i][3]))
    ends = [None, None, None, finish]
    for i in (3, 2, 1):
        _, c, d, _, e = maps[i]
        ends[i - 1] = add(add(mv(c, ends[i]), mv(d, fs[i])), e)
    enter, finish = fs[0], ends[0]
    for i in range(1, 4):
        enter = [jnp.where(mine == i, n, o) for n, o in zip(fs[i], enter)]
        finish = [jnp.where(mine == i, n, o) for n, o in zip(ends[i], finish)]
    return enter, finish


def finish_y(spot, near, far, values, ends, turned, parts, result, edge):
    me = spot[0:2, :]
    zero = [jnp.zeros((2, LANES), F32) for _ in range(3)]
    enter, finish = narrow(far, FAR_ORDER, me // 4, zero, zero)
    enter, finish = narrow(near, NEAR_ORDER, me % 4, enter, finish)
    f = enter
    inside = []
    for l in range(GROUPS):
        inside.append(f)
        for k in range(3):
            edge[pl.ds(k * 8 + l * 2, 2), :] = f[k]
        if l < GROUPS - 1:
            f = add(mv(quarter(parts, l, 0, 9), f), quarter(ends, l, 0, 3))
    a = finish
    for l in reversed(range(GROUPS)):
        for k in range(3):
            edge[pl.ds(24 + k * 8 + l * 2, 2), :] = a[k]
        if l > 0:
            a = add(
                add(mv(quarter(parts, l, 9, 9), a), mv(quarter(parts, l, 18, 9), inside[l])),
                quarter(ends, l, 3, 3),
            )
    f = [edge[pl.ds(k * 8, 8), :] for k in range(3)]
    a = [edge[pl.ds(24 + k * 8, 8), :] for k in range(3)]
    forward = []
    for y in range(8):
        f = add(mv([turned[y * 27 + k] for k in range(9)], f), [values[y * 3 + k] for k in range(3)])
        forward.append(f)
    solved = [None] * 8
    for y in reversed(range(8)):
        a = add(mv([turned[y * 27 + 18 + k] for k in range(9)], a), forward[y])
        solved[y] = a
    for k in range(3):
        rows = swap_blocks([solved[y][k] for y in range(8)])
        for x in range(8):
            for g in range(GROUPS):
                for half in range(2):
                    at = g * 2 + half
                    result[k, pl.ds(half * 8 + x, 1), g * LANES : (g + 1) * LANES] = rows[x][at : at + 1, :]


def body(pressure, exchange_rates, x_blocks, y_blocks, panels, outlet_tiles, outlet_counts, labels):
    shape = jax.ShapeDtypeStruct
    pressure, x_blocks, y_blocks = [jnp.transpose(v, (1, 0, 2)) for v in (pressure, x_blocks, y_blocks)]
    inputs = (pressure, exchange_rates, x_blocks, labels, panels, outlet_tiles, outlet_counts.reshape(1, 4))
    place = lax.axis_index("gy").astype(jnp.int32).reshape(1)
    packed, base = pl.pallas_call(
        prepare_x,
        out_shape=(shape((512, 256), BF16), shape((CX * 3, GROUPS, LANES), F32)),
        in_specs=[pl.BlockSpec(memory_space=pltpu.HBM)] * 7,
        out_specs=(VMEM,) * 2,
        scratch_shapes=[pltpu.VMEM(v.shape, v.dtype) for v in inputs]
        + [
            pltpu.SemaphoreType.DMA((7,)),
            pltpu.VMEM((1728, LANES), F32),
            pltpu.VMEM((512, LANES), F32),
            pltpu.VMEM((CX * 9, GROUPS, LANES), F32),
            pltpu.VMEM((1024, LANES), F32),
            pltpu.VMEM((16, 512), F32),
        ],
        name="prepare_x",
    )(*inputs)
    received = lax.all_to_all(packed, "gx", split_axis=0, concat_axis=0, tiled=True, axis_index_groups=LINE)
    turned, parts, whole, spot = pl.pallas_call(
        prepare_y,
        out_shape=(
            shape((8 * 27, 8, LANES), F32),
            shape((27 * 8, LANES), F32),
            shape((56, LANES), F32),
            shape((8, LANES), jnp.int32),
        ),
        in_specs=[SMEM, VMEM],
        out_specs=(VMEM,) * 4,
        scratch_shapes=[pltpu.VMEM((1728, LANES), F32), pltpu.VMEM((2048, LANES), F32)],
        compiler_params=PARAMS,
        name="prepare_y",
    )(place, y_blocks)
    received, whole = lax.optimization_barrier((received, whole))
    answer = pl.pallas_call(
        solve_x,
        out_shape=shape((512, LANES), BF16),
        in_specs=[VMEM],
        out_specs=VMEM,
        scratch_shapes=[
            pltpu.VMEM((512, LANES), F32),
            pltpu.VMEM((1024, LANES), F32),
            pltpu.VMEM((512, LANES), F32),
            pltpu.VMEM((512, LANES), F32),
            pltpu.VMEM((1024, LANES), F32),
        ],
        compiler_params=PARAMS,
        name="solve_x",
    )(received)
    entries = lax.all_to_all(answer, "gx", split_axis=0, concat_axis=0, tiled=True, axis_index_groups=LINE)
    sent, values, ends = pl.pallas_call(
        finish_x,
        out_shape=(
            shape((4 * ROWS, LANES), F32),
            shape((24, 8, LANES), F32),
            shape((48, LANES), F32),
        ),
        in_specs=[VMEM] * 6,
        out_specs=(VMEM,) * 3,
        scratch_shapes=[
            pltpu.VMEM((1728, LANES), F32),
            pltpu.VMEM((512, LANES), F32),
            pltpu.VMEM((256, LANES), F32),
            pltpu.VMEM((192, LANES), F32),
        ],
        compiler_params=PARAMS,
        name="finish_x",
    )(entries, base, x_blocks, turned, parts, whole)
    near = lax.all_to_all(sent, "gy", split_axis=0, concat_axis=0, tiled=True, axis_index_groups=NEAR)
    joined = pl.pallas_call(
        join_y,
        out_shape=shape((4 * ROWS, LANES), F32),
        in_specs=[VMEM],
        out_specs=VMEM,
        compiler_params=PARAMS,
        name="join_y",
    )(near)
    far = lax.all_to_all(joined, "gy", split_axis=0, concat_axis=0, tiled=True, axis_index_groups=FAR)
    result = pl.pallas_call(
        finish_y,
        out_shape=shape((3, CX, 512), F32),
        in_specs=[VMEM] * 7,
        out_specs=VMEM,
        scratch_shapes=[pltpu.VMEM((48, LANES), F32)],
        compiler_params=PARAMS,
        name="finish_y",
    )(spot, near, far, values, ends, turned, parts)
    return jnp.transpose(result, (1, 0, 2))


def solution(mesh):
    in_specs = (
        P("gx", None, "gy"),
        P("gx", None, "gy"),
        P("gx", None, "gy"),
        P("gx", None, "gy"),
        P(("gx", "gy"), None, None),
        P(("gx", "gy"), None),
        P(("gx", "gy")),
        P("gx", "gy"),
    )
    out_specs = P("gx", None, "gy")
    return jax.shard_map(body, mesh=mesh, in_specs=in_specs, out_specs=out_specs, check_vma=False)
```

```python
import jax
import jax.numpy as jnp
from jax import lax
from jax.experimental import pallas as pl
from jax.experimental.pallas import tpu as pltpu
from jax.sharding import PartitionSpec as P

F32 = jnp.float32
BF16 = jnp.bfloat16
CX, CY, NZ = 16, 32, 16
TX, TY = 32, 16
NEAR_ORDER, FAR_ORDER, TURN = (1, 2, 3, 0), (2, 1, 0, 3), 12
NEAR = [[4 * q + k for k in NEAR_ORDER] for q in range(4)]
FAR = [[4 * q + k for q in FAR_ORDER] for k in range(4)]
LINE = [[(i - TURN) % TX for i in range(TX)]]
ROWS = 72
LANES = 128
GROUPS = 4
MAP = 33
VMEM = pl.BlockSpec(memory_space=pltpu.VMEM)
SMEM = pl.BlockSpec(memory_space=pltpu.SMEM)
PARAMS = pltpu.CompilerParams(vmem_limit_bytes=32 * 1024 * 1024)


def mm(a, b):
    return [
        a[3 * r] * b[c] + a[3 * r + 1] * b[3 + c] + a[3 * r + 2] * b[6 + c]
        for r in range(3)
        for c in range(3)
    ]


def mv(a, v):
    return [a[3 * r] * v[0] + a[3 * r + 1] * v[1] + a[3 * r + 2] * v[2] for r in range(3)]


def add(a, b):
    return [x + y for x, y in zip(a, b)]


def iota(shape, axis):
    return lax.broadcasted_iota(jnp.int32, shape, axis)


def swap_blocks(parts):
    block = iota(parts[0].shape, 1) // NZ
    for bit in (1, 2, 4):
        low = (block & bit) == 0
        fresh = list(parts)
        for i in range(8):
            if i & bit == 0:
                first, second = parts[i], parts[i | bit]
                fresh[i] = jnp.where(low, first, pltpu.roll(second, bit * NZ, 1))
                fresh[i | bit] = jnp.where(low, pltpu.roll(first, LANES - bit * NZ, 1), second)
        parts = fresh
    return parts


def halves(g):
    return [((g * LANES + h * 64 + TURN * 16) % 512, slice(h * 64, h * 64 + 64)) for h in range(2)]


def in_order(ref, g, first):
    return jnp.concatenate([ref[at : at + 64, first : first + LANES].astype(F32) for at, _ in halves(g)], axis=0)


def load_blocks(blocks, coef):
    for k in range(27):
        rows = blocks[k].astype(F32)
        for g in range(GROUPS):
            coef[pl.ds(g * 432 + k * CX, CX), :] = rows[:, g * LANES : (g + 1) * LANES]


def x_matrix(coef, x, first):
    return [coef[pl.ds((first + k) * CX + x, GROUPS, stride=432), :] for k in range(9)]


def depth(v, z):
    up = jnp.where(z < NZ - 1, pltpu.roll(v, LANES - 1, 1) - v, 0.0)
    down = jnp.where(z > 0, v - pltpu.roll(v, 1, 1), 0.0)
    return up - down


def prepare_x(*refs):
    inputs, (packed, base) = refs[0:7], refs[7:9]
    buffers, arrived = refs[9:16], refs[16]
    coef, fields, prefix, feats, pan = refs[17:]
    copies = [pltpu.make_async_copy(inputs[k], buffers[k], arrived.at[k]) for k in range(7)]
    for copy in copies:
        copy.start()
    pressure, exchange, blocks, labels, panels, tiles, counts = buffers
    copies[0].wait()
    copies[1].wait()
    for g in range(GROUPS):
        cut = slice(g * LANES, (g + 1) * LANES)
        for k in range(3):
            fields[pl.ds(g * 128 + k * CX, CX), :] = pressure[k, :, cut]
        for x in range(CX):
            fields[pl.ds(g * 128 + 64 + x * 2, 2), :] = exchange[x, :, cut]
    z = iota((GROUPS, LANES), 1) & (NZ - 1)
    for x in range(CX):
        field = [fields[pl.ds(k * CX + x, GROUPS, stride=128), :] for k in range(3)]
        rates = [fields[pl.ds(64 + x * 2 + k, GROUPS, stride=128), :] for k in range(2)]
        inflow = rates[0] * (field[0] - field[1])
        outflow = rates[1] * (field[1] - field[2])
        base[x * 3] = field[0] - inflow + 0.2 * depth(field[0], z)
        base[x * 3 + 1] = field[1] + inflow - outflow + 0.2 * depth(field[1], z)
        base[x * 3 + 2] = field[2] + outflow + 0.2 * depth(field[2], z)
    for g in range(GROUPS):
        feats[pl.ds(g * 256 + 192, 64), :] = jnp.zeros((64, LANES), F32)
    copies[2].wait()
    load_blocks(blocks, coef)
    copies[3].wait()
    where_from = labels[...]
    where_from = (where_from // (TY * 4)) * 4 + (where_from & 3)
    where_from = where_from.astype(F32)
    for g in range(GROUPS):
        feats[pl.ds(g * 256 + 96, CX), :] = where_from[:, g * LANES : (g + 1) * LANES]

    u = x_matrix(coef, 0, 18)
    for x in range(1, CX):
        for k in range(9):
            prefix[x * 9 + k] = u[k]
        if x < CX - 1:
            u = mm(u, x_matrix(coef, x, 18))
    c_map = mm(u, x_matrix(coef, CX - 1, 18))

    def put(row, value):
        feats[pl.ds(row, GROUPS, stride=256), :] = value

    s, w = None, None
    b, e = None, None
    for x in reversed(range(CX)):
        ux = [prefix[x * 9 + k] for k in range(9)] if x > 0 else None
        if x == CX - 1:
            w = ux
        else:
            p = x_matrix(coef, x + 1, 0)
            s = p if s is None else mm(s, p)
            w = mm(w, p)
            if x > 0:
                w = add(w, ux)
            else:
                for k in (0, 4, 8):
                    w[k] = w[k] + 1.0
        gain = x_matrix(coef, x, 9)
        r = [base[x * 3 + k] for k in range(3)]
        column = [gain[0], gain[3], gain[6]]
        pushed = mv(gain, r)
        kb = column if s is None else mv(s, column)
        ke = mv(w, column)
        sb = pushed if s is None else mv(s, pushed)
        se = mv(w, pushed)
        b = sb if b is None else add(b, sb)
        e = se if e is None else add(e, se)
        for k in range(3):
            put(k * CX + x, kb[k])
            put((3 + k) * CX + x, ke[k])
    p = x_matrix(coef, 0, 0)
    values = mm(s, p) + c_map + mm(w, p) + b + e
    for k in range(MAP):
        high = values[k].astype(BF16).astype(F32)
        put(128 + k, high)
        put(128 + MAP + k, values[k] - high)

    for k in range(4, 7):
        copies[k].wait()
    for k in range(4):
        pan[pl.ds(k * 4, 4), :] = panels[k].astype(F32)
    row, column = iota((16, 4), 0), iota((16, 4), 1)
    listed = jnp.concatenate([jnp.broadcast_to(tiles[k : k + 1, :], (4, 4)) for k in range(4)], axis=0)
    limits = jnp.broadcast_to(counts[...], (16, 4))
    listed = jnp.sum(jnp.where(column == (row & 3), listed.astype(F32), 0.0), axis=1, keepdims=True)
    limits = jnp.sum(jnp.where(column == row // 4, limits.astype(F32), 0.0), axis=1, keepdims=True)
    routes = jnp.where((row[:, 0:1] & 3).astype(F32) < limits, listed, -1.0)
    routes = jnp.broadcast_to(routes, (16, LANES))
    routes = jnp.concatenate([routes] * 8, axis=0)
    lane = iota((LANES, LANES), 1)
    for g in range(GROUPS):
        slab = pan[:, g * LANES : (g + 1) * LANES]
        pieces = [pltpu.roll(slab, (112 - i * NZ) % LANES, 1) if i < 7 else slab for i in range(8)]
        first = feats[pl.ds(g * 256, LANES), :].T
        first = jnp.where(lane >= 112, jnp.concatenate(pieces, axis=0), first)
        for at, part in halves(g):
            packed[at : at + 64, 0:LANES] = first[part, :].astype(BF16)
        second = feats[pl.ds(g * 256 + LANES, LANES), :].T
        second = jnp.where(lane == 72, routes, second)
        for at, part in halves(g):
            packed[at : at + 64, LANES : 2 * LANES] = second[part, :].astype(BF16)


def solve_x(received, answer, low, high, spread, target, out):
    for g in range(GROUPS):
        rows = slice(g * LANES, (g + 1) * LANES)
        low[rows, :] = in_order(received, g, 0).T
        high[rows, :] = in_order(received, g, LANES).T
    r_id, c_id = iota((LANES, LANES), 0), iota((LANES, LANES), 1)
    lane = iota((512, LANES), 1)
    copy_panel = ((r_id >= 112) & ((r_id - 112) == (c_id & (NZ - 1)))).astype(F32).astype(BF16)
    copy_route = (r_id == 72).astype(F32).astype(BF16)
    panel_part = jnp.concatenate([in_order(received, g, 0) for g in range(GROUPS)], axis=0)
    panel_part = jnp.where(lane >= 112, panel_part, 0.0).astype(BF16)
    route_part = jnp.concatenate([in_order(received, g, LANES) for g in range(GROUPS)], axis=0)
    route_part = jnp.where(lane == 72, route_part, 0.0).astype(BF16)
    spread[...] = jnp.dot(panel_part, copy_panel, preferred_element_type=F32)
    target[...] = jnp.dot(route_part, copy_route, preferred_element_type=F32)
    tile_lane = (c_id // NZ).astype(F32)
    for g in range(GROUPS):
        table = None
        for j in range(4):
            hit = target[pl.ds(j, LANES, stride=4), :] == tile_lane + 8.0 * g
            part = jnp.where(hit, spread[pl.ds(j, LANES, stride=4), :], 0.0)
            table = part if table is None else table + part
        position = low[pl.ds(g * LANES + 96, CX), :].astype(jnp.int32)
        found = []
        for half in range(2):
            place = position[half * 8 : half * 8 + 8, :]
            inner, outer = place & 7, place // 8
            picked = jnp.zeros((8, LANES), F32)
            for o in range(16):
                chosen = jnp.take_along_axis(table[o * 8 : o * 8 + 8, :], inner, axis=0)
                picked = jnp.where(outer == o, chosen, picked)
            found.append(picked)
        source = jnp.concatenate(found, axis=0)
        out[pl.ds(g * LANES + 24, CX), :] = source
        for k in range(6):
            response = low[pl.ds(g * LANES + k * CX, CX), :]
            extra = jnp.sum(response * source, axis=0, keepdims=True)
            at = pl.ds(g * LANES + 27 + k, 1)
            high[at, :] = high[at, :] + extra

    def value(k):
        return high[pl.ds(k, 8, stride=LANES), :] + high[pl.ds(MAP + k, 8, stride=LANES), :]

    lanes8 = iota((8, LANES), 1)
    tile = iota((8, LANES), 0) * 8 + lanes8 // NZ

    def before(v, d, fill):
        if d < 8:
            turned = pltpu.roll(v, d * NZ, 1)
            moved = jnp.where(lanes8 >= d * NZ, turned, pltpu.roll(turned, 1, 0))
        else:
            moved = pltpu.roll(v, d // 8, 0)
        return jnp.where(tile >= d, moved, fill)

    def after(v, d, fill):
        if d < 8:
            turned = pltpu.roll(v, LANES - d * NZ, 1)
            moved = jnp.where(lanes8 < LANES - d * NZ, turned, pltpu.roll(turned, 7, 0))
        else:
            moved = pltpu.roll(v, 8 - d // 8, 0)
        return jnp.where(tile + d < TX, moved, fill)

    def scan(matrix, vector, shift):
        for d in (1, 2, 4, 8, 16):
            vector_now = add(mv(matrix, [shift(v, d, 0.0) for v in vector]), vector)
            if d < 16:
                matrix = mm(matrix, [shift(m, d, 1.0 if k in (0, 4, 8) else 0.0) for k, m in enumerate(matrix)])
            vector = vector_now
        return [shift(v, 1, 0.0) for v in vector]

    enter = scan([value(k) for k in range(9)], [value(27 + k) for k in range(3)], before)
    pushed = add(mv([value(18 + k) for k in range(9)], enter), [value(30 + k) for k in range(3)])
    finish = scan([value(9 + k) for k in range(9)], pushed, after)
    for k, v in enumerate(enter + finish):
        for piece in range(3):
            part = v.astype(BF16).astype(F32)
            out[pl.ds(piece * 6 + k, 8, stride=LANES), :] = part
            v = v - part
    for g in range(GROUPS):
        rows = slice(g * LANES, (g + 1) * LANES)
        turned_out = out[rows, :].T.astype(BF16)
        for at, part in halves(g):
            answer[at : at + 64, :] = turned_out[part, :]


def prepare_y(place, blocks, turned, parts, whole, spot, plain, coef):
    spot[...] = jnp.full((8, LANES), place[0], jnp.int32)
    load_blocks(blocks, plain)
    for half in range(2):
        for g in range(GROUPS):
            rows = swap_blocks([plain[pl.ds(g * 432 + half * 8 + i, 27, stride=CX), :] for i in range(8)])
            for y in range(8):
                coef[pl.ds((g * 2 + half) * 256 + y * 32, 27), :] = rows[y]
    phi, u, d_map = None, None, None
    for y in range(8):
        block = [coef[pl.ds(y * 32 + k, 8, stride=256), :] for k in range(27)]
        for k in range(27):
            turned[y * 27 + k] = block[k]
        phi = block[0:9] if y == 0 else mm(block[0:9], phi)
        d_map = phi if y == 0 else add(d_map, mm(u, phi))
        u = block[18:27] if y == 0 else mm(u, block[18:27])
    for k, v in enumerate(phi + u + d_map):
        parts[pl.ds(k * 8, 8), :] = v
    a, c, d = [quarter(parts, 0, 9 * k, 9) for k in range(3)]
    for l in range(1, GROUPS):
        a_l, c_l, d_l = [quarter(parts, l, 9 * k, 9) for k in range(3)]
        d = add(mm(mm(c, d_l), a), d)
        a = mm(a_l, a)
        c = mm(c, c_l)
    for k, v in enumerate(a + c + d):
        whole[pl.ds(k * 2, 2), :] = v
    whole[pl.ds(54, 2), :] = jnp.zeros((2, LANES), F32)


def quarter(ref, l, first, count):
    return [ref[pl.ds((first + k) * 8 + l * 2, 2), :] for k in range(count)]


def finish_x(received, base, blocks, turned, parts, whole, sent, values, ends, coef, low, stage, lined):
    load_blocks(blocks, coef)
    for g in range(GROUPS):
        rows = slice(g * LANES, (g + 1) * LANES)
        low[rows, :] = in_order(received, g, 0).T

    def entry(k):
        rows = [low[pl.ds(piece * 6 + k, GROUPS, stride=LANES), :] for piece in range(3)]
        return rows[0] + rows[1] + rows[2]

    f = [entry(k) for k in range(3)]
    a = [entry(3 + k) for k in range(3)]
    forward = []
    for x in range(CX):
        source = low[pl.ds(24 + x, GROUPS, stride=LANES), :]
        r = [base[x * 3] + source, base[x * 3 + 1], base[x * 3 + 2]]
        f = add(mv(x_matrix(coef, x, 0), f), mv(x_matrix(coef, x, 9), r))
        forward.append(f)
    for x in reversed(range(CX)):
        a = add(mv(x_matrix(coef, x, 18), a), forward[x])
        for k in range(3):
            stage[pl.ds(x * 16 + k * 4, 4), :] = a[k]
    for half in range(2):
        rows = swap_blocks([stage[pl.ds((half * 8 + i) * 16, 16), :] for i in range(8)])
        for y in range(8):
            for k in range(3):
                lined[pl.ds(half * 24 + y * 3 + k, 4, stride=48), :] = rows[y][k * 4 : k * 4 + 4, :]
    f, forward = None, []
    for y in range(8):
        r = [lined[pl.ds(y * 3 + k, 8, stride=24), :] for k in range(3)]
        pushed = mv([turned[y * 27 + 9 + k] for k in range(9)], r)
        for k in range(3):
            values[y * 3 + k] = pushed[k]
        f = pushed if f is None else add(mv([turned[y * 27 + k] for k in range(9)], f), pushed)
        forward.append(f)
    a = None
    for y in reversed(range(8)):
        a = forward[y] if a is None else add(mv([turned[y * 27 + 18 + k] for k in range(9)], a), forward[y])
    for k, v in enumerate(forward[7] + a):
        ends[pl.ds(k * 8, 8), :] = v
    enter, f = [], None
    for l in range(GROUPS):
        enter.append(f)
        b_l = quarter(ends, l, 0, 3)
        f = b_l if f is None else add(mv(quarter(parts, l, 0, 9), f), b_l)
    a = None
    for l in reversed(range(GROUPS)):
        now = quarter(ends, l, 3, 3)
        if enter[l] is not None:
            now = add(now, mv(quarter(parts, l, 18, 9), enter[l]))
        a = now if a is None else add(mv(quarter(parts, l, 9, 9), a), now)
    put_map(sent, [whole[pl.ds(k * 2, 2), :] for k in range(27)] + f + a)


def put_map(sent, values):
    for k, v in enumerate(values):
        sent[pl.ds(k * 2, 2), :] = v
    sent[pl.ds(66, 6), :] = jnp.zeros((6, LANES), F32)
    for i in range(1, 4):
        sent[pl.ds(i * ROWS, ROWS), :] = sent[pl.ds(0, ROWS), :]


def get_map(ref, order, i):
    i = order.index(i)
    v = [ref[pl.ds(i * ROWS + k * 2, 2), :] for k in range(MAP)]
    return v[0:9], v[9:18], v[18:27], v[27:30], v[30:33]


def join_y(received, sent):
    a, c, d, b, e = get_map(received, NEAR_ORDER, 0)
    for i in range(1, 4):
        a1, c1, d1, b1, e1 = get_map(received, NEAR_ORDER, i)
        e = add(mv(c, add(mv(d1, b), e1)), e)
        d = add(mm(c, mm(d1, a)), d)
        b = add(mv(a1, b), b1)
        a = mm(a1, a)
        c = mm(c, c1)
    put_map(sent, a + c + d + b + e)


def narrow(received, order, mine, enter, finish):
    maps = [get_map(received, order, i) for i in range(4)]
    fs = [enter]
    for i in range(3):
        fs.append(add(mv(maps[i][0], fs[i]), maps[i][3]))
    ends = [None, None, None, finish]
    for i in (3, 2, 1):
        _, c, d, _, e = maps[i]
        ends[i - 1] = add(add(mv(c, ends[i]), mv(d, fs[i])), e)
    enter, finish = fs[0], ends[0]
    for i in range(1, 4):
        enter = [jnp.where(mine == i, n, o) for n, o in zip(fs[i], enter)]
        finish = [jnp.where(mine == i, n, o) for n, o in zip(ends[i], finish)]
    return enter, finish


def finish_y(spot, near, far, values, ends, turned, parts, result, edge):
    me = spot[0:2, :]
    zero = [jnp.zeros((2, LANES), F32) for _ in range(3)]
    enter, finish = narrow(far, FAR_ORDER, me // 4, zero, zero)
    enter, finish = narrow(near, NEAR_ORDER, me % 4, enter, finish)
    f = enter
    inside = []
    for l in range(GROUPS):
        inside.append(f)
        for k in range(3):
            edge[pl.ds(k * 8 + l * 2, 2), :] = f[k]
        if l < GROUPS - 1:
            f = add(mv(quarter(parts, l, 0, 9), f), quarter(ends, l, 0, 3))
    a = finish
    for l in reversed(range(GROUPS)):
        for k in range(3):
            edge[pl.ds(24 + k * 8 + l * 2, 2), :] = a[k]
        if l > 0:
            a = add(
                add(mv(quarter(parts, l, 9, 9), a), mv(quarter(parts, l, 18, 9), inside[l])),
                quarter(ends, l, 3, 3),
            )
    f = [edge[pl.ds(k * 8, 8), :] for k in range(3)]
    a = [edge[pl.ds(24 + k * 8, 8), :] for k in range(3)]
    forward = []
    for y in range(8):
        f = add(mv([turned[y * 27 + k] for k in range(9)], f), [values[y * 3 + k] for k in range(3)])
        forward.append(f)
    solved = [None] * 8
    for y in reversed(range(8)):
        a = add(mv([turned[y * 27 + 18 + k] for k in range(9)], a), forward[y])
        solved[y] = a
    for k in range(3):
        rows = swap_blocks([solved[y][k] for y in range(8)])
        for x in range(8):
            for g in range(GROUPS):
                for half in range(2):
                    at = g * 2 + half
                    result[k, pl.ds(half * 8 + x, 1), g * LANES : (g + 1) * LANES] = rows[x][at : at + 1, :]


def body(pressure, exchange_rates, x_blocks, y_blocks, panels, outlet_tiles, outlet_counts, labels):
    shape = jax.ShapeDtypeStruct
    pressure, x_blocks, y_blocks = [jnp.transpose(v, (1, 0, 2)) for v in (pressure, x_blocks, y_blocks)]
    inputs = (pressure, exchange_rates, x_blocks, labels, panels, outlet_tiles, outlet_counts.reshape(1, 4))
    place = lax.axis_index("gy").astype(jnp.int32).reshape(1)
    packed, base = pl.pallas_call(
        prepare_x,
        out_shape=(shape((512, 256), BF16), shape((CX * 3, GROUPS, LANES), F32)),
        in_specs=[pl.BlockSpec(memory_space=pltpu.HBM)] * 7,
        out_specs=(VMEM,) * 2,
        scratch_shapes=[pltpu.VMEM(v.shape, v.dtype) for v in inputs]
        + [
            pltpu.SemaphoreType.DMA((7,)),
            pltpu.VMEM((1728, LANES), F32),
            pltpu.VMEM((512, LANES), F32),
            pltpu.VMEM((CX * 9, GROUPS, LANES), F32),
            pltpu.VMEM((1024, LANES), F32),
            pltpu.VMEM((16, 512), F32),
        ],
        name="prepare_x",
    )(*inputs)
    received = lax.all_to_all(packed, "gx", split_axis=0, concat_axis=0, tiled=True, axis_index_groups=LINE)
    turned, parts, whole, spot = pl.pallas_call(
        prepare_y,
        out_shape=(
            shape((8 * 27, 8, LANES), F32),
            shape((27 * 8, LANES), F32),
            shape((56, LANES), F32),
            shape((8, LANES), jnp.int32),
        ),
        in_specs=[SMEM, VMEM],
        out_specs=(VMEM,) * 4,
        scratch_shapes=[pltpu.VMEM((1728, LANES), F32), pltpu.VMEM((2048, LANES), F32)],
        compiler_params=PARAMS,
        name="prepare_y",
    )(place, y_blocks)
    received, whole = lax.optimization_barrier((received, whole))
    answer = pl.pallas_call(
        solve_x,
        out_shape=shape((512, LANES), BF16),
        in_specs=[VMEM],
        out_specs=VMEM,
        scratch_shapes=[
            pltpu.VMEM((512, LANES), F32),
            pltpu.VMEM((1024, LANES), F32),
            pltpu.VMEM((512, LANES), F32),
            pltpu.VMEM((512, LANES), F32),
            pltpu.VMEM((1024, LANES), F32),
        ],
        compiler_params=PARAMS,
        name="solve_x",
    )(received)
    entries = lax.all_to_all(answer, "gx", split_axis=0, concat_axis=0, tiled=True, axis_index_groups=LINE)
    sent, values, ends = pl.pallas_call(
        finish_x,
        out_shape=(
            shape((4 * ROWS, LANES), F32),
            shape((24, 8, LANES), F32),
            shape((48, LANES), F32),
        ),
        in_specs=[VMEM] * 6,
        out_specs=(VMEM,) * 3,
        scratch_shapes=[
            pltpu.VMEM((1728, LANES), F32),
            pltpu.VMEM((512, LANES), F32),
            pltpu.VMEM((256, LANES), F32),
            pltpu.VMEM((192, LANES), F32),
        ],
        compiler_params=PARAMS,
        name="finish_x",
    )(entries, base, x_blocks, turned, parts, whole)
    near = lax.all_to_all(sent, "gy", split_axis=0, concat_axis=0, tiled=True, axis_index_groups=NEAR)
    joined = pl.pallas_call(
        join_y,
        out_shape=shape((4 * ROWS, LANES), F32),
        in_specs=[VMEM],
        out_specs=VMEM,
        compiler_params=PARAMS,
        name="join_y",
    )(near)
    far = lax.all_to_all(joined, "gy", split_axis=0, concat_axis=0, tiled=True, axis_index_groups=FAR)
    result = pl.pallas_call(
        finish_y,
        out_shape=shape((3, CX, 512), F32),
        in_specs=[VMEM] * 7,
        out_specs=VMEM,
        scratch_shapes=[pltpu.VMEM((48, LANES), F32)],
        compiler_params=PARAMS,
        name="finish_y",
    )(spot, near, far, values, ends, turned, parts)
    return jnp.transpose(result, (1, 0, 2))


def solution(mesh):
    in_specs = (
        P("gx", None, "gy"),
        P("gx", None, "gy"),
        P("gx", None, "gy"),
        P("gx", None, "gy"),
        P(("gx", "gy"), None, None),
        P(("gx", "gy"), None),
        P(("gx", "gy")),
        P("gx", "gy"),
    )
    out_specs = P("gx", None, "gy")
    return jax.shard_map(body, mesh=mesh, in_specs=in_specs, out_specs=out_specs, check_vma=False)
```

```python
import jax
import jax.numpy as jnp
from jax import lax
from jax.experimental import pallas as pl
from jax.experimental.pallas import tpu as pltpu
from jax.sharding import PartitionSpec as P

F32 = jnp.float32
BF16 = jnp.bfloat16
CX, CY, NZ = 16, 32, 16
TX, TY = 32, 16
NEAR_ORDER, FAR_ORDER, TURN = (1, 2, 3, 0), (2, 1, 0, 3), 12
NEAR = [[4 * q + k for k in NEAR_ORDER] for q in range(4)]
FAR = [[4 * q + k for q in FAR_ORDER] for k in range(4)]
LINE = [[(i - TURN) % TX for i in range(TX)]]
ROWS = 72
LANES = 128
GROUPS = 4
MAP = 33
VMEM = pl.BlockSpec(memory_space=pltpu.VMEM)
SMEM = pl.BlockSpec(memory_space=pltpu.SMEM)
PARAMS = pltpu.CompilerParams(vmem_limit_bytes=32 * 1024 * 1024)


def mm(a, b):
    return [
        a[3 * r] * b[c] + a[3 * r + 1] * b[3 + c] + a[3 * r + 2] * b[6 + c]
        for r in range(3)
        for c in range(3)
    ]


def mv(a, v):
    return [a[3 * r] * v[0] + a[3 * r + 1] * v[1] + a[3 * r + 2] * v[2] for r in range(3)]


def add(a, b):
    return [x + y for x, y in zip(a, b)]


def iota(shape, axis):
    return lax.broadcasted_iota(jnp.int32, shape, axis)


def swap_blocks(parts):
    block = iota(parts[0].shape, 1) // NZ
    for bit in (1, 2, 4):
        low = (block & bit) == 0
        fresh = list(parts)
        for i in range(8):
            if i & bit == 0:
                first, second = parts[i], parts[i | bit]
                fresh[i] = jnp.where(low, first, pltpu.roll(second, bit * NZ, 1))
                fresh[i | bit] = jnp.where(low, pltpu.roll(first, LANES - bit * NZ, 1), second)
        parts = fresh
    return parts


def halves(g):
    return [((g * LANES + h * 64 + TURN * 16) % 512, slice(h * 64, h * 64 + 64)) for h in range(2)]


def in_order(ref, g, first):
    return jnp.concatenate([ref[at : at + 64, first : first + LANES].astype(F32) for at, _ in halves(g)], axis=0)


def load_blocks(blocks, coef):
    for k in range(27):
        rows = blocks[k].astype(F32)
        for g in range(GROUPS):
            coef[pl.ds(g * 432 + k * CX, CX), :] = rows[:, g * LANES : (g + 1) * LANES]


def x_matrix(coef, x, first):
    return [coef[pl.ds((first + k) * CX + x, GROUPS, stride=432), :] for k in range(9)]


def depth(v, z):
    up = jnp.where(z < NZ - 1, pltpu.roll(v, LANES - 1, 1) - v, 0.0)
    down = jnp.where(z > 0, v - pltpu.roll(v, 1, 1), 0.0)
    return up - down


def prepare_x(*refs):
    inputs, (packed, base) = refs[0:7], refs[7:9]
    buffers, arrived = refs[9:16], refs[16]
    coef, fields, prefix, feats, pan = refs[17:]
    copies = [pltpu.make_async_copy(inputs[k], buffers[k], arrived.at[k]) for k in range(7)]
    for copy in copies:
        copy.start()
    pressure, exchange, blocks, labels, panels, tiles, counts = buffers
    copies[0].wait()
    copies[1].wait()
    for g in range(GROUPS):
        cut = slice(g * LANES, (g + 1) * LANES)
        for k in range(3):
            fields[pl.ds(g * 128 + k * CX, CX), :] = pressure[k, :, cut]
        for x in range(CX):
            fields[pl.ds(g * 128 + 64 + x * 2, 2), :] = exchange[x, :, cut]
    z = iota((GROUPS, LANES), 1) & (NZ - 1)
    for x in range(CX):
        field = [fields[pl.ds(k * CX + x, GROUPS, stride=128), :] for k in range(3)]
        rates = [fields[pl.ds(64 + x * 2 + k, GROUPS, stride=128), :] for k in range(2)]
        inflow = rates[0] * (field[0] - field[1])
        outflow = rates[1] * (field[1] - field[2])
        base[x * 3] = field[0] - inflow + 0.2 * depth(field[0], z)
        base[x * 3 + 1] = field[1] + inflow - outflow + 0.2 * depth(field[1], z)
        base[x * 3 + 2] = field[2] + outflow + 0.2 * depth(field[2], z)
    for g in range(GROUPS):
        feats[pl.ds(g * 256 + 192, 64), :] = jnp.zeros((64, LANES), F32)
    copies[2].wait()
    load_blocks(blocks, coef)
    copies[3].wait()
    where_from = labels[...]
    where_from = (where_from // (TY * 4)) * 4 + (where_from & 3)
    where_from = where_from.astype(F32)
    for g in range(GROUPS):
        feats[pl.ds(g * 256 + 96, CX), :] = where_from[:, g * LANES : (g + 1) * LANES]

    u = x_matrix(coef, 0, 18)
    for x in range(1, CX):
        for k in range(9):
            prefix[x * 9 + k] = u[k]
        if x < CX - 1:
            u = mm(u, x_matrix(coef, x, 18))
    c_map = mm(u, x_matrix(coef, CX - 1, 18))

    def put(row, value):
        feats[pl.ds(row, GROUPS, stride=256), :] = value

    s, w = None, None
    b, e = None, None
    for x in reversed(range(CX)):
        ux = [prefix[x * 9 + k] for k in range(9)] if x > 0 else None
        if x == CX - 1:
            w = ux
        else:
            p = x_matrix(coef, x + 1, 0)
            s = p if s is None else mm(s, p)
            w = mm(w, p)
            if x > 0:
                w = add(w, ux)
            else:
                for k in (0, 4, 8):
                    w[k] = w[k] + 1.0
        gain = x_matrix(coef, x, 9)
        r = [base[x * 3 + k] for k in range(3)]
        column = [gain[0], gain[3], gain[6]]
        pushed = mv(gain, r)
        kb = column if s is None else mv(s, column)
        ke = mv(w, column)
        sb = pushed if s is None else mv(s, pushed)
        se = mv(w, pushed)
        b = sb if b is None else add(b, sb)
        e = se if e is None else add(e, se)
        for k in range(3):
            put(k * CX + x, kb[k])
            put((3 + k) * CX + x, ke[k])
    p = x_matrix(coef, 0, 0)
    values = mm(s, p) + c_map + mm(w, p) + b + e
    for k in range(MAP):
        high = values[k].astype(BF16).astype(F32)
        put(128 + k, high)
        put(128 + MAP + k, values[k] - high)

    for k in range(4, 7):
        copies[k].wait()
    for k in range(4):
        pan[pl.ds(k * 4, 4), :] = panels[k].astype(F32)
    row, column = iota((16, 4), 0), iota((16, 4), 1)
    listed = jnp.concatenate([jnp.broadcast_to(tiles[k : k + 1, :], (4, 4)) for k in range(4)], axis=0)
    limits = jnp.broadcast_to(counts[...], (16, 4))
    listed = jnp.sum(jnp.where(column == (row & 3), listed.astype(F32), 0.0), axis=1, keepdims=True)
    limits = jnp.sum(jnp.where(column == row // 4, limits.astype(F32), 0.0), axis=1, keepdims=True)
    routes = jnp.where((row[:, 0:1] & 3).astype(F32) < limits, listed, -1.0)
    routes = jnp.broadcast_to(routes, (16, LANES))
    routes = jnp.concatenate([routes] * 8, axis=0)
    lane = iota((LANES, LANES), 1)
    for g in range(GROUPS):
        slab = pan[:, g * LANES : (g + 1) * LANES]
        pieces = [pltpu.roll(slab, (112 - i * NZ) % LANES, 1) if i < 7 else slab for i in range(8)]
        first = feats[pl.ds(g * 256, LANES), :].T
        first = jnp.where(lane >= 112, jnp.concatenate(pieces, axis=0), first)
        for at, part in halves(g):
            packed[at : at + 64, 0:LANES] = first[part, :].astype(BF16)
        second = feats[pl.ds(g * 256 + LANES, LANES), :].T
        second = jnp.where(lane == 72, routes, second)
        for at, part in halves(g):
            packed[at : at + 64, LANES : 2 * LANES] = second[part, :].astype(BF16)


def solve_x(received, answer, low, high, spread, target, out):
    firsts = [in_order(received, g, 0) for g in range(GROUPS)]
    seconds = [in_order(received, g, LANES) for g in range(GROUPS)]
    for g in range(GROUPS):
        rows = slice(g * LANES, (g + 1) * LANES)
        low[rows, :] = firsts[g].T
        high[rows, :] = seconds[g].T
    r_id, c_id = iota((LANES, LANES), 0), iota((LANES, LANES), 1)
    lane = iota((512, LANES), 1)
    copy_panel = ((r_id >= 112) & ((r_id - 112) == (c_id & (NZ - 1)))).astype(F32).astype(BF16)
    copy_route = (r_id == 72).astype(F32).astype(BF16)
    panel_part = jnp.concatenate(firsts, axis=0)
    panel_part = jnp.where(lane >= 112, panel_part, 0.0).astype(BF16)
    route_part = jnp.concatenate(seconds, axis=0)
    route_part = jnp.where(lane == 72, route_part, 0.0).astype(BF16)
    spread[...] = jnp.dot(panel_part, copy_panel, preferred_element_type=F32)
    target[...] = jnp.dot(route_part, copy_route, preferred_element_type=F32)
    tile_lane = (c_id // NZ).astype(F32)
    for g in range(GROUPS):
        table = None
        for j in range(4):
            hit = target[pl.ds(j, LANES, stride=4), :] == tile_lane + 8.0 * g
            part = jnp.where(hit, spread[pl.ds(j, LANES, stride=4), :], 0.0)
            table = part if table is None else table + part
        position = low[pl.ds(g * LANES + 96, CX), :].astype(jnp.int32)
        found = []
        for half in range(2):
            place = position[half * 8 : half * 8 + 8, :]
            inner, outer = place & 7, place // 8
            picked = jnp.zeros((8, LANES), F32)
            for o in range(16):
                chosen = jnp.take_along_axis(table[o * 8 : o * 8 + 8, :], inner, axis=0)
                picked = jnp.where(outer == o, chosen, picked)
            found.append(picked)
        source = jnp.concatenate(found, axis=0)
        out[pl.ds(g * LANES + 24, CX), :] = source
        for k in range(6):
            response = low[pl.ds(g * LANES + k * CX, CX), :]
            extra = jnp.sum(response * source, axis=0, keepdims=True)
            at = pl.ds(g * LANES + 27 + k, 1)
            high[at, :] = high[at, :] + extra

    def value(k):
        return high[pl.ds(k, 8, stride=LANES), :] + high[pl.ds(MAP + k, 8, stride=LANES), :]

    lanes8 = iota((8, LANES), 1)
    tile = iota((8, LANES), 0) * 8 + lanes8 // NZ

    def before(v, d, fill):
        if d < 8:
            turned = pltpu.roll(v, d * NZ, 1)
            moved = jnp.where(lanes8 >= d * NZ, turned, pltpu.roll(turned, 1, 0))
        else:
            moved = pltpu.roll(v, d // 8, 0)
        return jnp.where(tile >= d, moved, fill)

    def after(v, d, fill):
        if d < 8:
            turned = pltpu.roll(v, LANES - d * NZ, 1)
            moved = jnp.where(lanes8 < LANES - d * NZ, turned, pltpu.roll(turned, 7, 0))
        else:
            moved = pltpu.roll(v, 8 - d // 8, 0)
        return jnp.where(tile + d < TX, moved, fill)

    def scan(matrix, vector, shift):
        for d in (1, 2, 4, 8, 16):
            vector_now = add(mv(matrix, [shift(v, d, 0.0) for v in vector]), vector)
            if d < 16:
                matrix = mm(matrix, [shift(m, d, 1.0 if k in (0, 4, 8) else 0.0) for k, m in enumerate(matrix)])
            vector = vector_now
        return [shift(v, 1, 0.0) for v in vector]

    enter = scan([value(k) for k in range(9)], [value(27 + k) for k in range(3)], before)
    pushed = add(mv([value(18 + k) for k in range(9)], enter), [value(30 + k) for k in range(3)])
    finish = scan([value(9 + k) for k in range(9)], pushed, after)
    for k, v in enumerate(enter + finish):
        for piece in range(3):
            part = v.astype(BF16).astype(F32)
            out[pl.ds(piece * 6 + k, 8, stride=LANES), :] = part
            v = v - part
    for g in range(GROUPS):
        rows = slice(g * LANES, (g + 1) * LANES)
        turned_out = out[rows, :].T.astype(BF16)
        for at, part in halves(g):
            answer[at : at + 64, :] = turned_out[part, :]


def prepare_y(place, blocks, turned, parts, whole, spot, plain, coef):
    spot[...] = jnp.full((8, LANES), place[0], jnp.int32)
    load_blocks(blocks, plain)
    for half in range(2):
        for g in range(GROUPS):
            rows = swap_blocks([plain[pl.ds(g * 432 + half * 8 + i, 27, stride=CX), :] for i in range(8)])
            for y in range(8):
                coef[pl.ds((g * 2 + half) * 256 + y * 32, 27), :] = rows[y]
    phi, u, d_map = None, None, None
    for y in range(8):
        block = [coef[pl.ds(y * 32 + k, 8, stride=256), :] for k in range(27)]
        for k in range(27):
            turned[y * 27 + k] = block[k]
        phi = block[0:9] if y == 0 else mm(block[0:9], phi)
        d_map = phi if y == 0 else add(d_map, mm(u, phi))
        u = block[18:27] if y == 0 else mm(u, block[18:27])
    for k, v in enumerate(phi + u + d_map):
        parts[pl.ds(k * 8, 8), :] = v
    a, c, d = [quarter(parts, 0, 9 * k, 9) for k in range(3)]
    for l in range(1, GROUPS):
        a_l, c_l, d_l = [quarter(parts, l, 9 * k, 9) for k in range(3)]
        d = add(mm(mm(c, d_l), a), d)
        a = mm(a_l, a)
        c = mm(c, c_l)
    for k, v in enumerate(a + c + d):
        whole[pl.ds(k * 2, 2), :] = v
    whole[pl.ds(54, 2), :] = jnp.zeros((2, LANES), F32)


def quarter(ref, l, first, count):
    return [ref[pl.ds((first + k) * 8 + l * 2, 2), :] for k in range(count)]


def finish_x(received, base, blocks, turned, parts, whole, sent, values, ends, coef, low, stage, lined):
    load_blocks(blocks, coef)
    for g in range(GROUPS):
        rows = slice(g * LANES, (g + 1) * LANES)
        low[rows, :] = in_order(received, g, 0).T

    def entry(k):
        rows = [low[pl.ds(piece * 6 + k, GROUPS, stride=LANES), :] for piece in range(3)]
        return rows[0] + rows[1] + rows[2]

    f = [entry(k) for k in range(3)]
    a = [entry(3 + k) for k in range(3)]
    forward = []
    for x in range(CX):
        source = low[pl.ds(24 + x, GROUPS, stride=LANES), :]
        r = [base[x * 3] + source, base[x * 3 + 1], base[x * 3 + 2]]
        f = add(mv(x_matrix(coef, x, 0), f), mv(x_matrix(coef, x, 9), r))
        forward.append(f)
    for x in reversed(range(CX)):
        a = add(mv(x_matrix(coef, x, 18), a), forward[x])
        for k in range(3):
            stage[pl.ds(x * 16 + k * 4, 4), :] = a[k]
    for half in range(2):
        rows = swap_blocks([stage[pl.ds((half * 8 + i) * 16, 16), :] for i in range(8)])
        for y in range(8):
            for k in range(3):
                lined[pl.ds(half * 24 + y * 3 + k, 4, stride=48), :] = rows[y][k * 4 : k * 4 + 4, :]
    f, forward = None, []
    for y in range(8):
        r = [lined[pl.ds(y * 3 + k, 8, stride=24), :] for k in range(3)]
        pushed = mv([turned[y * 27 + 9 + k] for k in range(9)], r)
        for k in range(3):
            values[y * 3 + k] = pushed[k]
        f = pushed if f is None else add(mv([turned[y * 27 + k] for k in range(9)], f), pushed)
        forward.append(f)
    a = None
    for y in reversed(range(8)):
        a = forward[y] if a is None else add(mv([turned[y * 27 + 18 + k] for k in range(9)], a), forward[y])
    for k, v in enumerate(forward[7] + a):
        ends[pl.ds(k * 8, 8), :] = v
    enter, f = [], None
    for l in range(GROUPS):
        enter.append(f)
        b_l = quarter(ends, l, 0, 3)
        f = b_l if f is None else add(mv(quarter(parts, l, 0, 9), f), b_l)
    a = None
    for l in reversed(range(GROUPS)):
        now = quarter(ends, l, 3, 3)
        if enter[l] is not None:
            now = add(now, mv(quarter(parts, l, 18, 9), enter[l]))
        a = now if a is None else add(mv(quarter(parts, l, 9, 9), a), now)
    put_map(sent, [whole[pl.ds(k * 2, 2), :] for k in range(27)] + f + a)


def put_map(sent, values):
    for k, v in enumerate(values):
        sent[pl.ds(k * 2, 2), :] = v
    sent[pl.ds(66, 6), :] = jnp.zeros((6, LANES), F32)
    for i in range(1, 4):
        sent[pl.ds(i * ROWS, ROWS), :] = sent[pl.ds(0, ROWS), :]


def get_map(ref, order, i):
    i = order.index(i)
    v = [ref[pl.ds(i * ROWS + k * 2, 2), :] for k in range(MAP)]
    return v[0:9], v[9:18], v[18:27], v[27:30], v[30:33]


def join_y(received, sent):
    a, c, d, b, e = get_map(received, NEAR_ORDER, 0)
    for i in range(1, 4):
        a1, c1, d1, b1, e1 = get_map(received, NEAR_ORDER, i)
        e = add(mv(c, add(mv(d1, b), e1)), e)
        d = add(mm(c, mm(d1, a)), d)
        b = add(mv(a1, b), b1)
        a = mm(a1, a)
        c = mm(c, c1)
    put_map(sent, a + c + d + b + e)


def narrow(received, order, mine, enter, finish):
    maps = [get_map(received, order, i) for i in range(4)]
    fs = [enter]
    for i in range(3):
        fs.append(add(mv(maps[i][0], fs[i]), maps[i][3]))
    ends = [None, None, None, finish]
    for i in (3, 2, 1):
        _, c, d, _, e = maps[i]
        ends[i - 1] = add(add(mv(c, ends[i]), mv(d, fs[i])), e)
    enter, finish = fs[0], ends[0]
    for i in range(1, 4):
        enter = [jnp.where(mine == i, n, o) for n, o in zip(fs[i], enter)]
        finish = [jnp.where(mine == i, n, o) for n, o in zip(ends[i], finish)]
    return enter, finish


def finish_y(spot, near, far, values, ends, turned, parts, result, edge):
    me = spot[0:2, :]
    zero = [jnp.zeros((2, LANES), F32) for _ in range(3)]
    enter, finish = narrow(far, FAR_ORDER, me // 4, zero, zero)
    enter, finish = narrow(near, NEAR_ORDER, me % 4, enter, finish)
    f = enter
    inside = []
    for l in range(GROUPS):
        inside.append(f)
        for k in range(3):
            edge[pl.ds(k * 8 + l * 2, 2), :] = f[k]
        if l < GROUPS - 1:
            f = add(mv(quarter(parts, l, 0, 9), f), quarter(ends, l, 0, 3))
    a = finish
    for l in reversed(range(GROUPS)):
        for k in range(3):
            edge[pl.ds(24 + k * 8 + l * 2, 2), :] = a[k]
        if l > 0:
            a = add(
                add(mv(quarter(parts, l, 9, 9), a), mv(quarter(parts, l, 18, 9), inside[l])),
                quarter(ends, l, 3, 3),
            )
    f = [edge[pl.ds(k * 8, 8), :] for k in range(3)]
    a = [edge[pl.ds(24 + k * 8, 8), :] for k in range(3)]
    forward = []
    for y in range(8):
        f = add(mv([turned[y * 27 + k] for k in range(9)], f), [values[y * 3 + k] for k in range(3)])
        forward.append(f)
    solved = [None] * 8
    for y in reversed(range(8)):
        a = add(mv([turned[y * 27 + 18 + k] for k in range(9)], a), forward[y])
        solved[y] = a
    for k in range(3):
        rows = swap_blocks([solved[y][k] for y in range(8)])
        for x in range(8):
            for g in range(GROUPS):
                for half in range(2):
                    at = g * 2 + half
                    result[k, pl.ds(half * 8 + x, 1), g * LANES : (g + 1) * LANES] = rows[x][at : at + 1, :]


def body(pressure, exchange_rates, x_blocks, y_blocks, panels, outlet_tiles, outlet_counts, labels):
    shape = jax.ShapeDtypeStruct
    pressure, x_blocks, y_blocks = [jnp.transpose(v, (1, 0, 2)) for v in (pressure, x_blocks, y_blocks)]
    inputs = (pressure, exchange_rates, x_blocks, labels, panels, outlet_tiles, outlet_counts.reshape(1, 4))
    place = lax.axis_index("gy").astype(jnp.int32).reshape(1)
    packed, base = pl.pallas_call(
        prepare_x,
        out_shape=(shape((512, 256), BF16), shape((CX * 3, GROUPS, LANES), F32)),
        in_specs=[pl.BlockSpec(memory_space=pltpu.HBM)] * 7,
        out_specs=(VMEM,) * 2,
        scratch_shapes=[pltpu.VMEM(v.shape, v.dtype) for v in inputs]
        + [
            pltpu.SemaphoreType.DMA((7,)),
            pltpu.VMEM((1728, LANES), F32),
            pltpu.VMEM((512, LANES), F32),
            pltpu.VMEM((CX * 9, GROUPS, LANES), F32),
            pltpu.VMEM((1024, LANES), F32),
            pltpu.VMEM((16, 512), F32),
        ],
        name="prepare_x",
    )(*inputs)
    received = lax.all_to_all(packed, "gx", split_axis=0, concat_axis=0, tiled=True, axis_index_groups=LINE)
    turned, parts, whole, spot = pl.pallas_call(
        prepare_y,
        out_shape=(
            shape((8 * 27, 8, LANES), F32),
            shape((27 * 8, LANES), F32),
            shape((56, LANES), F32),
            shape((8, LANES), jnp.int32),
        ),
        in_specs=[SMEM, VMEM],
        out_specs=(VMEM,) * 4,
        scratch_shapes=[pltpu.VMEM((1728, LANES), F32), pltpu.VMEM((2048, LANES), F32)],
        compiler_params=PARAMS,
        name="prepare_y",
    )(place, y_blocks)
    received, whole = lax.optimization_barrier((received, whole))
    answer = pl.pallas_call(
        solve_x,
        out_shape=shape((512, LANES), BF16),
        in_specs=[VMEM],
        out_specs=VMEM,
        scratch_shapes=[
            pltpu.VMEM((512, LANES), F32),
            pltpu.VMEM((1024, LANES), F32),
            pltpu.VMEM((512, LANES), F32),
            pltpu.VMEM((512, LANES), F32),
            pltpu.VMEM((1024, LANES), F32),
        ],
        compiler_params=PARAMS,
        name="solve_x",
    )(received)
    entries = lax.all_to_all(answer, "gx", split_axis=0, concat_axis=0, tiled=True, axis_index_groups=LINE)
    sent, values, ends = pl.pallas_call(
        finish_x,
        out_shape=(
            shape((4 * ROWS, LANES), F32),
            shape((24, 8, LANES), F32),
            shape((48, LANES), F32),
        ),
        in_specs=[VMEM] * 6,
        out_specs=(VMEM,) * 3,
        scratch_shapes=[
            pltpu.VMEM((1728, LANES), F32),
            pltpu.VMEM((512, LANES), F32),
            pltpu.VMEM((256, LANES), F32),
            pltpu.VMEM((192, LANES), F32),
        ],
        compiler_params=PARAMS,
        name="finish_x",
    )(entries, base, x_blocks, turned, parts, whole)
    near = lax.all_to_all(sent, "gy", split_axis=0, concat_axis=0, tiled=True, axis_index_groups=NEAR)
    joined = pl.pallas_call(
        join_y,
        out_shape=shape((4 * ROWS, LANES), F32),
        in_specs=[VMEM],
        out_specs=VMEM,
        compiler_params=PARAMS,
        name="join_y",
    )(near)
    far = lax.all_to_all(joined, "gy", split_axis=0, concat_axis=0, tiled=True, axis_index_groups=FAR)
    result = pl.pallas_call(
        finish_y,
        out_shape=shape((3, CX, 512), F32),
        in_specs=[VMEM] * 7,
        out_specs=VMEM,
        scratch_shapes=[pltpu.VMEM((48, LANES), F32)],
        compiler_params=PARAMS,
        name="finish_y",
    )(spot, near, far, values, ends, turned, parts)
    return jnp.transpose(result, (1, 0, 2))


def solution(mesh):
    in_specs = (
        P("gx", None, "gy"),
        P("gx", None, "gy"),
        P("gx", None, "gy"),
        P("gx", None, "gy"),
        P(("gx", "gy"), None, None),
        P(("gx", "gy"), None),
        P(("gx", "gy")),
        P("gx", "gy"),
    )
    out_specs = P("gx", None, "gy")
    return jax.shard_map(body, mesh=mesh, in_specs=in_specs, out_specs=out_specs, check_vma=False)
```
